32 devices in a mesh: ctx: 8 (over z, y), fsdp: 4 (over x, core).
Axes of the slice: x: 2, y: 2, z: 4, core: 2. Of those that a mesh axis runs over, the one named last changes fastest.
Arguments:
- tokens: bfloat16 [4, 2048, 1024], P('fsdp', 'ctx'), may hold values from -6 to 6
- cotangent: bfloat16 [4, 2048, 1024], P('fsdp', 'ctx'), may hold values from -6 to 6
- positions: int32 [4, 2048], P('fsdp', 'ctx'), may hold values from 0 to 4095, as said below
- block_order: int32 [4, 16], P('fsdp'), may hold values from 0 to 15, as said below
- joint_weight: bfloat16 [1024, 3072], P('fsdp'), may hold values from -0.1875 to 0.1875
- joint_bias: bfloat16 [3072], P('fsdp'), may hold values from -3 to 3
- dense_weight: bfloat16 [1024, 1024], P('fsdp'), may hold values from -4 to 4
- dense_bias: bfloat16 [1024], P('fsdp'), may hold values from -2 to 2
- inner_weight: bfloat16 [1024, 4096], P('fsdp'), may hold values from -0.1875 to 0.1875
- inner_bias: bfloat16 [4096], P('fsdp'), may hold values from -3 to 3
- outer_weight: bfloat16 [4096, 1024], P('fsdp'), may hold values from -0.09375 to 0.09375
- outer_bias: bfloat16 [1024], P('fsdp'), may hold values from -2 to 2
- attention_gain: bfloat16 [1024], P('fsdp'), may hold values from 0.5 to 1.5
- attention_shift: bfloat16 [1024], P('fsdp'), may hold values from -2 to 2
- feedforward_gain: bfloat16 [1024], P('fsdp'), may hold values from 0.5 to 1.5
- feedforward_shift: bfloat16 [1024], P('fsdp'), may hold values from -2 to 2
Outputs:
- layer_output: bfloat16 [4, 2048, 1024], P('fsdp', 'ctx')
- tokens_grad: bfloat16 [4, 2048, 1024], P('fsdp', 'ctx')
- joint_weight_grad: float32 [1024, 3072], P('fsdp')
- joint_bias_grad: float32 [3072], P('fsdp')
- dense_weight_grad: float32 [1024, 1024], P('fsdp')
- dense_bias_grad: float32 [1024], P('fsdp')
- inner_weight_grad: float32 [1024, 4096], P('fsdp')
- inner_bias_grad: float32 [4096], P('fsdp')
- outer_weight_grad: float32 [4096, 1024], P('fsdp')
- outer_bias_grad: float32 [1024], P('fsdp')
- attention_gain_grad: float32 [1024], P('fsdp')
- attention_shift_grad: float32 [1024], P('fsdp')
- feedforward_gain_grad: float32 [1024], P('fsdp')
- feedforward_shift_grad: float32 [1024], P('fsdp')
The draws below stay inside these ranges and needn't reach their ends.
Inputs may be any that keep to these rules, and one draw needn't show every extreme that they name: `block_order`: row i lists, for the 16 stored blocks of 128 tokens of sequence i, the causal block that each holds; every number of 0 to 15 stands once in a row. `positions`: the token of causal index j has rotary position 2 j or 2 j + 1.
All inputs are finite; a program needn't handle non-finite values.
Results may differ from the reference program's by a relative error of at most 0.018.
Values may be sent and summed in bfloat16 or wider, within the bound.
No kernel may reach another device: no remote copies, remote signals or barrier semaphores. Data moves between devices by JAX's collectives and lax.ppermute only.
A program may use at most 384 MiB of HBM per device.

```python
import math
import jax
import jax.numpy as jnp
from jax import lax

D = 1024
H = 16
DH = 64
ROT = 16
FF = 4096
SEQ_LEN = 2048
NBLK = 16
BLK = 128
SEQS = 4


def block_tables(key):
    table_key = jax.random.fold_in(key, 5)
    row_keys = jax.random.split(table_key, SEQS)
    tables = jax.vmap(lambda one_key: jax.random.permutation(one_key, NBLK))(row_keys)
    return tables.astype(jnp.int32)


def draw_block_order(key, part):
    return block_tables(key)


def draw_positions(key, part):
    tables = block_tables(key)
    key = jax.random.fold_in(key, 7)
    coin_bits = jax.random.randint(key, (SEQS, SEQ_LEN), 0, 2, dtype=jnp.int32)
    indices = jnp.arange(SEQ_LEN, dtype=jnp.int32)
    coin_bits = jnp.where(indices[None, :] == 0, 0, coin_bits)
    coin_bits = jnp.where(indices[None, :] == SEQ_LEN - 1, 1, coin_bits)
    causal_pos = 2 * indices[None, :] + coin_bits
    block_ids = jnp.broadcast_to((indices // BLK)[None, :], (SEQS, SEQ_LEN))
    causal = jnp.take_along_axis(tables, block_ids, axis=1) * BLK + indices[None, :] % BLK
    return jnp.take_along_axis(causal_pos, causal, axis=1).astype(jnp.int32)


def steps_of(key, shape, cuts, low, largest):
    def one(axis_at, blocks):
        steps = jax.random.uniform(jax.random.fold_in(jax.random.fold_in(key, 6), axis_at), (blocks,), jnp.float32, low / len(cuts), largest / len(cuts))
        return jnp.repeat(jnp.exp(steps), shape[axis_at] // blocks).reshape((-1,) + (1,) * (len(shape) - axis_at - 1))

    gain = one(*cuts[0])
    for cut in cuts[1:]:
        gain = gain * one(*cut)
    return gain


def scatter_about(rng, dims, spread, reach, cuts=(), kind=jnp.bfloat16):
    values = spread * jax.random.normal(rng, dims, jnp.float32)
    if cuts:
        values = values * steps_of(rng, dims, cuts, -0.22, 0.18)
    return jnp.clip(values, -reach, reach).astype(kind)


def setup_inputs(seed: int = 0) -> dict:
    keys = jax.random.split(jax.random.key(seed), 17)
    return {
        "tokens": scatter_about(keys[0], (SEQS, SEQ_LEN, D), 1.0, 6.0, ((0, 4), (1, 8))),
        "cotangent": scatter_about(keys[1], (SEQS, SEQ_LEN, D), 1.0, 6.0, ((0, 4), (1, 8))),
        "positions": draw_positions(jax.random.fold_in(keys[16], 71), 0),
        "block_order": draw_block_order(jax.random.fold_in(keys[16], 71), 0),
        "joint_weight": scatter_about(keys[4], (D, 3 * D), D ** -0.5, 0.1875, ((0, 4),)),
        "joint_bias": scatter_about(keys[5], (3 * D,), 0.5, 3.0, ((0, 4),)),
        "dense_weight": scatter_about(keys[6], (D, D), (max(1, 4 * D // SEQ_LEN)) ** -0.5, 4.0, ((0, 4),)),
        "dense_bias": scatter_about(keys[7], (D,), 0.3, 2.0, ((0, 4),)),
        "inner_weight": scatter_about(keys[8], (D, FF), D ** -0.5, 0.1875, ((0, 4),)),
        "inner_bias": scatter_about(keys[9], (FF,), 0.5, 3.0, ((0, 4),)),
        "outer_weight": scatter_about(keys[10], (FF, D), FF ** -0.5, 0.09375, ((0, 4),)),
        "outer_bias": scatter_about(keys[11], (D,), 0.3, 2.0, ((0, 4),)),
        "attention_gain": jnp.clip(1.0 + 0.1 * jax.random.normal(keys[12], (D,), jnp.float32), 0.5, 1.5).astype(jnp.bfloat16),
        "attention_shift": scatter_about(keys[13], (D,), 0.3, 2.0, ((0, 4),)),
        "feedforward_gain": jnp.clip(1.0 + 0.1 * jax.random.normal(keys[14], (D,), jnp.float32), 0.5, 1.5).astype(jnp.bfloat16),
        "feedforward_shift": scatter_about(keys[15], (D,), 0.3, 2.0, ((0, 4),)),
    }


EPSILON = 1e-05
MASKED = -1e+30
HIGHEST = lax.Precision.HIGHEST

@jax.custom_vjp
def low(v):
    return lax.optimization_barrier(v.astype(jnp.bfloat16)).astype(jnp.float32)

@jax.custom_vjp
def low_back(v):
    return v

def low_keep(v):
    return (low(v), None)

def low_pass(kept, grad):
    return (grad,)

def back_keep(v):
    return (v, None)

def back_low(kept, grad):
    return (low(grad),)
low.defvjp(low_keep, low_pass)
low_back.defvjp(back_keep, back_low)

def layer_norm(inputs, norm_gain, norm_shift):
    row_mean = lax.optimization_barrier(jnp.mean(inputs, axis=-1, keepdims=True))
    centered = inputs - row_mean
    variance = lax.optimization_barrier(jnp.mean(centered * centered, axis=-1, keepdims=True))
    return centered * lax.rsqrt(variance + EPSILON) * norm_gain + norm_shift

def angles(token_pos):
    exponent = jnp.arange(0, ROT, 2).astype(jnp.float32) / ROT
    inverse = 10000.0 ** (-exponent)
    phases = token_pos.astype(jnp.float32)[:, None] * inverse[None, :]
    phases = jnp.concatenate([phases, phases], axis=1)[:, None, :]
    return (jnp.cos(phases), jnp.sin(phases))

def rotate(heads, cosine, sine):
    half_rot = ROT // 2
    first_half = heads[..., :half_rot]
    second_half = heads[..., half_rot:ROT]
    turned = jnp.concatenate([-second_half, first_half], axis=-1)
    rotated = heads[..., :ROT] * cosine + turned * sine
    return jnp.concatenate([rotated, heads[..., ROT:]], axis=-1)

def attend(query, key_heads, value_heads, causal):
    length = query.shape[0]
    block_rows = math.gcd(length, 512)
    count = length // block_rows
    query_blocks = query.reshape(count, block_rows, H, DH)
    causal_blocks = causal.reshape(count, block_rows)
    scale = DH ** (-0.5)

    def one_block(record):
        query_block, causal_block = record
        scores = low_back(jnp.einsum('qhd,khd->hqk', query_block, key_heads, precision=HIGHEST) * scale)
        allowed = causal_block[:, None] >= causal[None, :]
        scores = jnp.where(allowed[None], scores, MASKED)
        row_top = lax.optimization_barrier(jnp.max(scores, axis=-1, keepdims=True))
        exp_scores = jnp.exp(scores - row_top)
        probs = low(exp_scores / lax.optimization_barrier(jnp.sum(exp_scores, axis=-1, keepdims=True)))
        return jnp.einsum('hqk,khd->qhd', probs, value_heads, precision=HIGHEST)
    mixed = lax.map(jax.checkpoint(one_block), (query_blocks, causal_blocks))
    return mixed.reshape(length, H * DH)

def one_sequence(inputs, token_pos, block_table, weights):
    joint_weight, joint_bias, dense_weight, dense_bias, inner_weight, inner_bias, outer_weight, outer_bias, attention_gain, attention_shift, feedforward_gain, feedforward_shift = weights
    length = inputs.shape[0]
    places = jnp.arange(length, dtype=jnp.int32)
    block_len = length // NBLK
    causal = block_table[places // block_len] * block_len + places % block_len
    hidden_attn = low(layer_norm(inputs, attention_gain, attention_shift))
    hidden_ff = low(layer_norm(inputs, feedforward_gain, feedforward_shift))
    joint = low_back(jnp.dot(hidden_attn, joint_weight, precision=HIGHEST) + joint_bias)
    joint = joint.reshape(length, H, 3, DH)
    cosine, sine = angles(token_pos)
    query = low(rotate(joint[:, :, 0], cosine, sine))
    key_heads = low(rotate(joint[:, :, 1], cosine, sine))
    value_heads = low(joint[:, :, 2])
    mixed = low_back(low(attend(query, key_heads, value_heads, causal)))
    attention_out = jnp.dot(mixed, dense_weight, precision=HIGHEST) + dense_bias
    inner = low_back(jnp.dot(hidden_ff, inner_weight, precision=HIGHEST) + inner_bias)
    activated = low(jax.nn.gelu(inner, approximate=False))
    outer = jnp.dot(activated, outer_weight, precision=HIGHEST) + outer_bias
    return inputs + attention_out + outer

def reference(tokens, cotangent, positions, block_order, joint_weight, joint_bias, dense_weight, dense_bias, inner_weight, inner_bias, outer_weight, outer_bias, attention_gain, attention_shift, feedforward_gain, feedforward_shift):
    weights = (joint_weight.astype(jnp.float32), joint_bias.astype(jnp.float32), dense_weight.astype(jnp.float32), dense_bias.astype(jnp.float32), inner_weight.astype(jnp.float32), inner_bias.astype(jnp.float32), outer_weight.astype(jnp.float32), outer_bias.astype(jnp.float32), attention_gain.astype(jnp.float32), attention_shift.astype(jnp.float32), feedforward_gain.astype(jnp.float32), feedforward_shift.astype(jnp.float32))
    inputs = tokens.astype(jnp.float32)
    upstream = cotangent.astype(jnp.float32)

    def forward(inputs, weights):

        def advance(running, record):
            return (running, one_sequence(record[0], record[1], record[2], weights))
        running, outputs = lax.scan(advance, None, (inputs, positions, block_order))
        return outputs
    outputs, pullback = jax.vjp(forward, inputs, weights)
    inputs_grad, grads = pullback(upstream)
    joint_weight_grad, joint_bias_grad, dense_weight_grad, dense_bias_grad, inner_weight_grad, inner_bias_grad, outer_weight_grad, outer_bias_grad, attention_gain_grad, attention_shift_grad, feedforward_gain_grad, feedforward_shift_grad = grads
    return (outputs.astype(jnp.bfloat16), inputs_grad.astype(jnp.bfloat16), joint_weight_grad, joint_bias_grad, dense_weight_grad, dense_bias_grad, inner_weight_grad, inner_bias_grad, outer_weight_grad, outer_bias_grad, attention_gain_grad, attention_shift_grad, feedforward_gain_grad, feedforward_shift_grad)
```

```python
import functools
import math

import jax
import jax.numpy as jnp
from jax import lax
from jax.experimental import pallas as pl
from jax.experimental.pallas import tpu as pltpu
from jax.sharding import PartitionSpec as P

D = 1024
H = 16
DH = 64
ROT = 16
PAIR = 2 * DH
EPSILON = 1e-05
MASKED = -1e30
SCALE = DH ** (-0.5)
LOG2E = math.log2(math.e)
BF16 = jnp.bfloat16
F32 = jnp.float32
MIB = 1024 * 1024
FF_RING = True


def dot(left, right, left_dim=1, right_dim=0):
    return lax.dot_general(
        left, right, (((left_dim,), (right_dim,)), ((), ())), preferred_element_type=F32
    )


def ring_order(count):
    return list(range(0, count, 2)) + list(range(1, count, 2))[::-1]


def ring_steps(axis, count):
    order = ring_order(count)
    onward = [(order[k], order[(k + 1) % count]) for k in range(count)]
    back = [(b, a) for a, b in onward]
    places = [0] * count
    for place, index in enumerate(order):
        places[index] = place
    place = jnp.array(places, jnp.int32)[lax.axis_index(axis)]
    return onward, back, place


def ring_reduce(pick, axis, count):
    onward, back, place = ring_steps(axis, count)
    half = count // 2
    far = pick((place + half) % count)
    rows = far.shape[0] // 2
    up = lax.ppermute(far[:rows], axis, onward)
    down = lax.ppermute(far[rows:], axis, back)
    for step in range(2, half + 1):
        mine_up = pick((place + half - step + 1) % count)
        mine_down = pick((place + count - half + step - 1) % count)
        if step == 2:
            mine_up = jnp.concatenate([mine_up[:rows] + up, mine_up[rows:]], axis=0)
            mine_down = jnp.concatenate([mine_down[:rows], mine_down[rows:] + down], axis=0)
        else:
            mine_up = mine_up + up
            mine_down = mine_down + down
        up = lax.ppermute(mine_up, axis, onward)
        down = lax.ppermute(mine_down, axis, back)
    own = pick(place).astype(F32)
    return (own + up.astype(F32) + down.astype(F32)).astype(BF16)


def ring_gather(own, axis, count, place_chunk, state):
    onward, back, place = ring_steps(axis, count)
    half = count // 2
    rows = own.shape[0] // 2
    state = place_chunk(state, own, place, 0)
    up = down = own
    for step in range(1, half):
        up = lax.ppermute(up, axis, onward)
        down = lax.ppermute(down, axis, back)
        state = place_chunk(state, up, (place + count - step) % count, 0)
        state = place_chunk(state, down, (place + step) % count, 0)
    up = lax.ppermute(up[:rows], axis, onward)
    down = lax.ppermute(down[rows:], axis, back)
    return place_chunk(state, jnp.concatenate([up, down], axis=0), (place + half) % count, 0)


def gather_pairs(own, count):
    if count != 4:
        return lax.all_gather(own, "fsdp", axis=0)
    index = lax.axis_index("fsdp")
    across = lax.ppermute(own, "fsdp", [(k, k ^ 2) for k in range(4)])
    first = index < 2
    pair = jnp.stack([jnp.where(first, own, across), jnp.where(first, across, own)])
    other = lax.ppermute(pair, "fsdp", [(k, k ^ 1) for k in range(4)])
    even = index % 2 == 0
    return jnp.stack([jnp.where(even, pair, other), jnp.where(even, other, pair)], axis=1).reshape(
        (4,) + own.shape
    )


def turn(heads, cosine, sine):
    lane = lax.broadcasted_iota(jnp.int32, heads.shape, 1) % DH
    partner = jnp.where(
        lane < ROT // 2,
        pltpu.roll(heads, PAIR - ROT // 2, 1),
        pltpu.roll(heads, ROT // 2, 1),
    )
    return heads * cosine + partner * sine


def project_kernel(hidden_ref, weight_ref, bias_ref, upstream_ref, dense_ref, cos_ref, sin_ref, out_ref):
    joint = dot(hidden_ref[...], weight_ref[...]) + bias_ref[...].astype(F32)
    low = lax.broadcasted_iota(jnp.int32, (joint.shape[0], PAIR), 1) < DH
    one, two, three = joint[:, :PAIR], joint[:, PAIR : 2 * PAIR], joint[:, 2 * PAIR :]
    query = jnp.where(low, one, two)
    key = pltpu.roll(jnp.where(low, three, one), DH, 1)
    value = jnp.where(low, two, three)
    cosine, sine = cos_ref[...], sin_ref[...]
    out_ref[0, :, :PAIR] = turn(query, cosine, sine).astype(BF16)
    out_ref[0, :, PAIR : 2 * PAIR] = turn(key, cosine, sine).astype(BF16)
    out_ref[0, :, 2 * PAIR : 3 * PAIR] = value.astype(BF16)
    out_ref[0, :, 3 * PAIR :] = dot(upstream_ref[...], dense_ref[...], 1, 1).astype(BF16)


def project(hidden, weight, bias, upstream, dense, cosine, sine, seqs, tokens, pairs):
    return pl.pallas_call(
        project_kernel,
        grid=(seqs, pairs),
        in_specs=[
            pl.BlockSpec((tokens, D), lambda s, p: (s, 0)),
            pl.BlockSpec((D, 3 * PAIR), lambda s, p: (0, p)),
            pl.BlockSpec((1, 3 * PAIR), lambda s, p: (0, p)),
            pl.BlockSpec((tokens, D), lambda s, p: (s, 0)),
            pl.BlockSpec((PAIR, D), lambda s, p: (p, 0)),
            pl.BlockSpec((tokens, PAIR), lambda s, p: (s, 0)),
            pl.BlockSpec((tokens, PAIR), lambda s, p: (s, 0)),
        ],
        out_specs=pl.BlockSpec((1, tokens, 4 * PAIR), lambda s, p: (s * pairs + p, 0, 0)),
        out_shape=jax.ShapeDtypeStruct((seqs * pairs, tokens, 4 * PAIR), BF16),
        compiler_params=pltpu.CompilerParams(vmem_limit_bytes=40 * MIB),
        cost_estimate=pl.CostEstimate(
            flops=2 * seqs * pairs * tokens * D * 4 * PAIR,
            bytes_accessed=10 * MIB,
            transcendentals=0,
        ),
        name="project",
    )(hidden, weight, bias, upstream, dense, cosine, sine)


def unturn_kernel(back_ref, cos_ref, sin_ref, grad_ref, mixed_ref):
    cosine, sine = cos_ref[...], sin_ref[...]
    query = turn(back_ref[0, :, PAIR : 2 * PAIR].astype(F32), cosine, -sine)
    key = turn(back_ref[0, :, 2 * PAIR : 3 * PAIR].astype(F32), cosine, -sine)
    value = back_ref[0, :, 3 * PAIR :].astype(F32)
    low = lax.broadcasted_iota(jnp.int32, query.shape, 1) < DH
    key = pltpu.roll(key, DH, 1)
    grad_ref[:, :PAIR] = jnp.where(low, query, key).astype(BF16)
    grad_ref[:, PAIR : 2 * PAIR] = jnp.where(low, value, query).astype(BF16)
    grad_ref[:, 2 * PAIR :] = jnp.where(low, key, value).astype(BF16)
    mixed_ref[...] = back_ref[0, :, :PAIR]


def unturn(back, cosine, sine, seqs, tokens, pairs):
    return pl.pallas_call(
        unturn_kernel,
        grid=(seqs, pairs),
        in_specs=[
            pl.BlockSpec((1, tokens, 4 * PAIR), lambda s, p: (s * pairs + p, 0, 0)),
            pl.BlockSpec((tokens, PAIR), lambda s, p: (s, 0)),
            pl.BlockSpec((tokens, PAIR), lambda s, p: (s, 0)),
        ],
        out_specs=[
            pl.BlockSpec((tokens, 3 * PAIR), lambda s, p: (s, p)),
            pl.BlockSpec((tokens, PAIR), lambda s, p: (s, p)),
        ],
        out_shape=[
            jax.ShapeDtypeStruct((seqs * tokens, pairs * 3 * PAIR), BF16),
            jax.ShapeDtypeStruct((seqs * tokens, pairs * PAIR), BF16),
        ],
        compiler_params=pltpu.CompilerParams(vmem_limit_bytes=32 * MIB),
        cost_estimate=pl.CostEstimate(flops=8 * MIB, bytes_accessed=5 * MIB, transcendentals=0),
        name="unturn",
    )(back, cosine, sine)


def attend_kernel(tile, block, unrolled, order_ref, in_ref, out_ref, sorted_ref, flipped_ref,
                  score_ref, prob_ref, mixed_ref, dq_ref, dk_ref, dv_ref):
    head = pl.program_id(0)
    length = in_ref.shape[0]
    tiles = length // tile
    blocks = length // block

    def loop(count, body, carry):
        if unrolled:
            for index in range(count):
                carry = body(index, carry)
            return carry
        return lax.fori_loop(0, count, body, carry)

    def span(index, size):
        start = index * size
        if not isinstance(start, int):
            start = pl.multiple_of(start, size)
        return pl.ds(start, size)

    @pl.when(head == 0)
    def prepare():
        def one(index, carry):
            sorted_ref[span(order_ref[index], block), :] = in_ref[span(index, block), :]
            return carry

        loop(blocks, one, 0)

        def flip(index, carry):
            flipped_ref[:, span(index, tile)] = sorted_ref[span(index, tile), :].T
            return carry

        loop(tiles, flip, 0)
        dk_ref[...] = jnp.zeros_like(dk_ref)
        dv_ref[...] = jnp.zeros_like(dv_ref)

    first = pl.multiple_of(head * DH, DH)

    def padded(rows):
        rows = rows.astype(F32)
        zero = jnp.zeros_like(rows)
        upper = jnp.where(head == 0, rows, zero)
        lower = jnp.where(head == 0, zero, rows)
        return jnp.concatenate([upper, lower], axis=0).astype(BF16)

    def one_tile(i, carry):
        query = padded(flipped_ref[pl.ds(first, DH), span(i, tile)])

        def score(j, top):
            part = dot(sorted_ref[span(j, tile), PAIR : 2 * PAIR], query)
            if not (unrolled and j < i):
                keys = j * tile + lax.broadcasted_iota(jnp.int32, part.shape, 0)
                queries = i * tile + lax.broadcasted_iota(jnp.int32, part.shape, 1)
                part = jnp.where(keys <= queries, part, MASKED)
            score_ref[span(j, tile), :] = part
            return jnp.maximum(top, jnp.max(part, axis=0, keepdims=True))

        top = loop(i + 1, score, jnp.full((1, tile), -3e38, F32))
        shift = top * (SCALE * LOG2E)

        def mix(j, status):
            total, mixed = status
            prob = jnp.exp2(score_ref[span(j, tile), :] * (SCALE * LOG2E) - shift)
            low = prob.astype(BF16)
            prob_ref[span(j, tile), :] = low
            total = total + jnp.sum(prob, axis=0, keepdims=True)
            values = flipped_ref[pl.ds(2 * PAIR + first, DH), span(j, tile)]
            return total, mixed + dot(values, low)

        total, mixed = loop(
            i + 1, mix, (jnp.zeros((1, tile), F32), jnp.zeros((DH, tile), F32))
        )
        inverse = 1.0 / total
        mixed = mixed * inverse
        mixed_ref[pl.ds(first, DH), span(i, tile)] = mixed
        grad = flipped_ref[pl.ds(3 * PAIR + first, DH), span(i, tile)].astype(F32) * inverse
        grad = grad.astype(BF16)
        delta = jnp.sum(grad.astype(F32) * mixed, axis=0, keepdims=True)
        grad = padded(grad)

        def pull(j, dq):
            low = prob_ref[span(j, tile), :]
            prob_grad = dot(sorted_ref[span(j, tile), 2 * PAIR : 3 * PAIR], grad)
            score_grad = (low.astype(F32) * (prob_grad - delta)).astype(BF16)
            dv_ref[span(j, tile), :] += dot(low, grad, 1, 1)
            dk_ref[span(j, tile), :] += dot(score_grad, query, 1, 1)
            keys = flipped_ref[pl.ds(PAIR + first, DH), span(j, tile)]
            return dq + dot(keys, score_grad)

        dq_ref[pl.ds(first, DH), span(i, tile)] = loop(i + 1, pull, jnp.zeros((DH, tile), F32))
        return carry

    loop(tiles, one_tile, 0)

    @pl.when(head == pl.num_programs(0) - 1)
    def finish():
        def one(index, carry):
            source = span(order_ref[index], block)
            target = span(index, block)
            out_ref[target, :PAIR] = mixed_ref[:, source].T.astype(BF16)
            out_ref[target, PAIR : 2 * PAIR] = (dq_ref[:, source].T * SCALE).astype(BF16)
            out_ref[target, 2 * PAIR : 3 * PAIR] = (dk_ref[source, :] * SCALE).astype(BF16)
            out_ref[target, 3 * PAIR :] = dv_ref[source, :].astype(BF16)
            return carry

        loop(blocks, one, 0)


def attend(order, packed, block):
    length = packed.shape[0]
    unrolled = length <= 2048
    tile = 256 if unrolled else 128
    return pl.pallas_call(
        functools.partial(attend_kernel, tile, block, unrolled),
        grid=(2,),
        in_specs=[
            pl.BlockSpec(memory_space=pltpu.SMEM),
            pl.BlockSpec(memory_space=pltpu.VMEM),
        ],
        out_specs=pl.BlockSpec(memory_space=pltpu.VMEM),
        out_shape=jax.ShapeDtypeStruct((length, 4 * PAIR), BF16),
        scratch_shapes=[
            pltpu.VMEM((length, 4 * PAIR), BF16),
            pltpu.VMEM((4 * PAIR, length), BF16),
            pltpu.VMEM((length, tile), F32),
            pltpu.VMEM((length, tile), BF16),
            pltpu.VMEM((PAIR, length), F32),
            pltpu.VMEM((PAIR, length), F32),
            pltpu.VMEM((length, PAIR), F32),
            pltpu.VMEM((length, PAIR), F32),
        ],
        compiler_params=pltpu.CompilerParams(
            vmem_limit_bytes=(40 if unrolled else 60) * MIB,
            dimension_semantics=("arbitrary",),
        ),
        cost_estimate=pl.CostEstimate(
            flops=16 * length * length * PAIR, bytes_accessed=4 * MIB, transcendentals=0
        ),
        name="attend",
    )(order, packed)


def exact_gelu(values):
    return jax.nn.gelu(values, approximate=False)


def rotary_tables(token_pos):
    lane = jnp.arange(PAIR, dtype=jnp.int32) % DH
    exponent = (2 * (lane % (ROT // 2))).astype(F32) / ROT
    inverse = 10000.0 ** (-exponent)
    phases = token_pos[:, None] * inverse[None, :]
    turned = (lane < ROT)[None, :]
    sign = jnp.where(lane < ROT // 2, -1.0, 1.0)[None, :]
    return jnp.where(turned, jnp.cos(phases), 1.0), jnp.where(turned, jnp.sin(phases) * sign, 0.0)


def per_device(ctx, fsdp, tokens, cotangent, positions, block_order, joint_weight, joint_bias,
               dense_weight, dense_bias, inner_weight, inner_bias, outer_weight, outer_bias,
               attention_gain, attention_shift, feedforward_gain, feedforward_shift):
    seqs = fsdp
    count = tokens.shape[1]
    block = count // 2
    rows = joint_weight.shape[0]
    heads = H // fsdp
    pairs = heads // 2
    joint_cols = heads * 3 * DH
    inner_cols = inner_weight.shape[1] // fsdp
    all_tokens = seqs * count
    me = lax.axis_index("ctx")

    pos = positions[0]
    table = block_order[0].astype(BF16)
    extra = jnp.concatenate(
        [
            attention_gain, attention_shift, feedforward_gain, feedforward_shift,
            dense_bias, outer_bias, (pos // 128).astype(BF16), (pos % 128).astype(BF16),
            table, jnp.zeros((14 * D - table.shape[0],), BF16),
        ]
    ).reshape(16, D)
    payload = gather_pairs(jnp.concatenate([tokens[0], extra], axis=0), fsdp)
    joint_local = lax.all_to_all(
        joint_weight.reshape(rows, fsdp, joint_cols).transpose(1, 0, 2), "fsdp", 0, 0
    ).reshape(D, joint_cols)
    upstream = gather_pairs(cotangent[0], fsdp).reshape(all_tokens, D)
    inner_local = lax.all_to_all(
        inner_weight.reshape(rows, fsdp, inner_cols).transpose(1, 0, 2), "fsdp", 0, 0
    ).reshape(D, inner_cols)

    inputs = payload[:, :count].reshape(all_tokens, D).astype(F32)
    params = payload[:, count].reshape(fsdp, 4, rows).transpose(1, 0, 2).reshape(4, D).astype(F32)
    second = payload[:, count + 1].astype(F32)
    bias_sum = second[:, :rows].reshape(D) + second[:, rows : 2 * rows].reshape(D)
    token_pos = (second[:, 2 * rows : 2 * rows + count] * 128.0
                 + second[:, 2 * rows + count : 2 * rows + 2 * count]).reshape(all_tokens)
    tables = payload[:, count + 2, : table.shape[0]].astype(jnp.int32)

    row_mean = jnp.mean(inputs, axis=-1, keepdims=True)
    centered = inputs - row_mean
    spread = lax.rsqrt(jnp.mean(centered * centered, axis=-1, keepdims=True) + EPSILON)
    normed = centered * spread
    hidden_attn = (normed * params[0] + params[1]).astype(BF16)
    hidden_ff = (normed * params[2] + params[3]).astype(BF16)
    cosine, sine = rotary_tables(token_pos)

    sent = project(hidden_attn, joint_local, joint_bias[None], upstream, dense_weight, cosine, sine,
                   seqs, count, pairs)
    jobs = seqs * pairs
    if ctx > jobs:
        sent = jnp.concatenate([sent] * (ctx // jobs), axis=0)
        each = 1
    else:
        each = jobs // ctx
    got = lax.all_to_all(sent.reshape(ctx, each, count, 4 * PAIR), "ctx", 0, 0)

    inner = dot(hidden_ff, inner_local) + inner_bias.astype(F32)
    activated, pull_gelu = jax.vjp(exact_gelu, inner)
    activated = activated.astype(BF16)
    inner_grad = pull_gelu(dot(upstream, outer_weight, 1, 1))[0].astype(BF16)
    outer_weight_grad = dot(activated, upstream, 0, 0).astype(BF16)
    inner_weight_grad = dot(hidden_ff, inner_grad, 0, 0).astype(BF16)
    inner_bias_grad = jnp.sum(inner_grad.astype(F32), axis=0)
    hidden_ff_grad = dot(inner_grad, inner_local, 1, 1)
    ff_out = dot(activated, outer_weight)

    per = rows // ctx
    outer_rows = outer_weight.shape[0] // ctx
    ff_terms = jnp.concatenate(
        [
            outer_weight_grad.reshape(ctx, outer_rows, D),
            inner_weight_grad.reshape(fsdp, ctx, per, inner_cols).transpose(1, 0, 2, 3).reshape(
                ctx, fsdp * per, inner_cols
            ),
        ],
        axis=1,
    )

    def place_ff(state, chunk, number, part):
        outer_state, inner_state = state
        outer_state = lax.dynamic_update_slice_in_dim(
            outer_state, chunk[:outer_rows].astype(F32), number * outer_rows, 0
        )
        wide = chunk[outer_rows:].reshape(fsdp, per, inner_cols).transpose(1, 0, 2)
        inner_state = lax.dynamic_update_slice_in_dim(
            inner_state, wide.reshape(per, -1).astype(F32), number * per, 0
        )
        return outer_state, inner_state

    if FF_RING:
        ff_own = ring_reduce(
            lambda k: lax.dynamic_index_in_dim(ff_terms, k, 0, keepdims=False), "ctx", ctx
        )
    else:
        ff_own = lax.psum_scatter(ff_terms, "ctx", scatter_dimension=0)
    inner_own = lax.all_to_all(
        ff_own[outer_rows:].reshape(fsdp, per, inner_cols), "fsdp", 0, 0
    ).reshape(-1, inner_cols)
    ff_own = jnp.concatenate([ff_own[:outer_rows], inner_own], axis=0)
    if FF_RING:
        outer_total, inner_total = ring_gather(
            ff_own, "ctx", ctx, place_ff,
            (jnp.zeros(outer_weight.shape, F32), jnp.zeros(inner_weight.shape, F32)),
        )
    else:
        ff_all = lax.all_gather(ff_own, "ctx", axis=0)
        outer_total = ff_all[:, :outer_rows].reshape(-1, D).astype(F32)
        inner_total = ff_all[:, outer_rows:].reshape(ctx, fsdp, per, inner_cols).transpose(
            0, 2, 1, 3).reshape(rows, -1).astype(F32)

    backs = []
    for k in range(each):
        sequence = (lax.rem(me, jobs) * each + k) // pairs if ctx <= jobs else lax.rem(me, jobs) // pairs
        order = lax.dynamic_index_in_dim(tables, sequence, 0, keepdims=False)
        backs.append(attend(order, got[:, k].reshape(ctx * count, 4 * PAIR), block))
    back = jnp.stack([b.reshape(ctx, count, 4 * PAIR) for b in backs], axis=1)
    back = lax.all_to_all(back, "ctx", 0, 0)[: max(1, jobs // each)]
    joint_grad, mixed = unturn(
        back.reshape(jobs, count, 4 * PAIR), cosine, sine, seqs, count, pairs
    )

    out_part = (ff_out + dot(mixed, dense_weight)).astype(BF16)
    hidden_attn_grad = dot(joint_grad, joint_local, 1, 1)
    e_part = (params[0] * hidden_attn_grad + params[2] * hidden_ff_grad).astype(BF16)
    parts = lax.all_to_all(
        jnp.concatenate([out_part.reshape(seqs, count, D), e_part.reshape(seqs, count, D)], axis=1),
        "fsdp", 0, 0,
    )

    dense_weight_grad = dot(mixed, upstream, 0, 0).astype(BF16)
    joint_weight_grad = dot(hidden_attn, joint_grad, 0, 0).astype(BF16)
    joint_bias_grad = jnp.sum(joint_grad.astype(F32), axis=0)
    upstream_grad = jnp.sum(upstream.astype(F32), axis=0)

    gains = jnp.stack(
        [
            jnp.sum(hidden_attn_grad * normed, axis=0),
            jnp.sum(hidden_attn_grad, axis=0),
            jnp.sum(hidden_ff_grad * normed, axis=0),
            jnp.sum(hidden_ff_grad, axis=0),
        ]
    ).astype(BF16)
    lanes = 2 * PAIR
    gains = gains.reshape(4, fsdp, ctx, per).transpose(2, 1, 0, 3).reshape(ctx, fsdp, 4 * per)
    gains = jnp.pad(gains, ((0, 0), (0, 0), (0, lanes - 4 * per)))
    my_rows = lax.dynamic_slice_in_dim(
        upstream_grad, lax.axis_index("fsdp") * rows, rows, 0
    )
    small = jnp.concatenate(
        [joint_bias_grad.reshape(ctx, -1), inner_bias_grad.reshape(ctx, -1), my_rows.reshape(ctx, -1)],
        axis=1,
    ).astype(BF16)
    small = jnp.pad(small[:, None], ((0, 0), (0, 31 - fsdp), (0, lanes - small.shape[1])))
    joint_blocks, dense_blocks = joint_cols // lanes, D // lanes
    terms = jnp.concatenate(
        [
            joint_weight_grad.reshape(fsdp, ctx, per, joint_blocks, lanes)
            .transpose(1, 0, 3, 2, 4).reshape(ctx, -1, lanes),
            dense_weight_grad.reshape(ctx, per, dense_blocks, lanes)
            .transpose(0, 2, 1, 3).reshape(ctx, -1, lanes),
            gains,
            small,
        ],
        axis=1,
    )
    own = ring_reduce(lambda k: lax.dynamic_index_in_dim(terms, k, 0, keepdims=False), "ctx", ctx)
    joint_rows = fsdp * joint_blocks * per
    dense_rows = dense_blocks * per
    after = joint_rows + dense_rows
    exchanged = jnp.concatenate(
        [
            own[:joint_rows].reshape(fsdp, joint_blocks * per, lanes),
            jnp.pad(own[after : after + fsdp][:, None], ((0, 0), (0, 15), (0, 0))),
        ],
        axis=1,
    )
    exchanged = lax.all_to_all(exchanged, "fsdp", 0, 0)
    gain_own = jnp.sum(exchanged[:, joint_blocks * per].astype(F32), axis=0).astype(BF16)
    own = jnp.concatenate(
        [
            exchanged[:, : joint_blocks * per].reshape(joint_rows, lanes),
            own[joint_rows:after],
            jnp.pad(gain_own[None], ((0, fsdp - 1), (0, 0))),
            own[after + fsdp :],
        ],
        axis=0,
    )

    def place_late(state, chunk, number, part):
        joint_state, dense_state, vectors = state
        wide = chunk[:joint_rows].reshape(fsdp, joint_blocks, per, lanes).transpose(2, 0, 1, 3)
        joint_state = lax.dynamic_update_slice_in_dim(
            joint_state, wide.reshape(per, -1).astype(F32), number * per, 0
        )
        wide = chunk[joint_rows:after].reshape(dense_blocks, per, lanes).transpose(1, 0, 2)
        dense_state = lax.dynamic_update_slice_in_dim(
            dense_state, wide.reshape(per, -1).astype(F32), number * per, 0
        )
        pieces = jnp.stack([chunk[after + fsdp], chunk[after]])[None]
        vectors = lax.dynamic_update_slice_in_dim(vectors, pieces.astype(F32), number, 0)
        return joint_state, dense_state, vectors

    joint_total, dense_total, vectors = ring_gather(
        own, "ctx", ctx, place_late,
        (jnp.zeros(joint_weight.shape, F32), jnp.zeros(dense_weight.shape, F32),
         jnp.zeros((ctx, 2, lanes), F32)),
    )
    a, b = joint_cols // ctx, inner_cols // ctx
    joint_bias_total = vectors[:, 0, :a].reshape(-1)
    inner_bias_total = vectors[:, 0, a : a + b].reshape(-1)
    upstream_total = vectors[:, 0, a + b : a + b + per].reshape(-1)
    gain_totals = [vectors[:, 1, k * per : (k + 1) * per].reshape(-1) for k in range(4)]

    layer_output = (tokens[0].astype(F32) + bias_sum
                    + jnp.sum(parts[:, :count].astype(F32), axis=0)).astype(BF16)
    e = jnp.sum(parts[:, count:].astype(F32), axis=0)
    mine = tokens[0].astype(F32)
    mine_centered = mine - jnp.mean(mine, axis=-1, keepdims=True)
    mine_spread = lax.rsqrt(jnp.mean(mine_centered * mine_centered, axis=-1, keepdims=True) + EPSILON)
    mine_normed = mine_centered * mine_spread
    tokens_grad = (
        cotangent[0].astype(F32)
        + (e - jnp.mean(e, axis=-1, keepdims=True)
           - mine_normed * jnp.mean(e * mine_normed, axis=-1, keepdims=True)) * mine_spread
    ).astype(BF16)

    return (
        layer_output[None], tokens_grad[None],
        joint_total, joint_bias_total, dense_total, upstream_total,
        inner_total, inner_bias_total, outer_total, upstream_total,
        gain_totals[0], gain_totals[1], gain_totals[2], gain_totals[3],
    )


def solution(mesh):
    tokens = P("fsdp", "ctx", None)
    weight = P("fsdp", None)
    vector = P("fsdp")
    return jax.shard_map(
        functools.partial(per_device, mesh.shape["ctx"], mesh.shape["fsdp"]),
        mesh=mesh,
        in_specs=(tokens, tokens, P("fsdp", "ctx"), weight) + (weight, vector) * 4 + (vector,) * 4,
        out_specs=(tokens, tokens) + (weight, vector) * 4 + (vector,) * 4,
        check_vma=False,
    )
```

```python
import functools
import math

import jax
import jax.numpy as jnp
from jax import lax
from jax.experimental import pallas as pl
from jax.experimental.pallas import tpu as pltpu
from jax.sharding import PartitionSpec as P

D = 1024
H = 16
DH = 64
ROT = 16
PAIR = 2 * DH
EPSILON = 1e-05
MASKED = -1e30
SCALE = DH ** (-0.5)
LOG2E = math.log2(math.e)
BF16 = jnp.bfloat16
F32 = jnp.float32
MIB = 1024 * 1024


def dot(left, right, left_dim=1, right_dim=0):
    return lax.dot_general(
        left, right, (((left_dim,), (right_dim,)), ((), ())), preferred_element_type=F32
    )


def ring_order(count):
    return list(range(0, count, 2)) + list(range(1, count, 2))[::-1]


def ring_steps(axis, count):
    order = ring_order(count)
    onward = [(order[k], order[(k + 1) % count]) for k in range(count)]
    back = [(b, a) for a, b in onward]
    places = [0] * count
    for place, index in enumerate(order):
        places[index] = place
    place = jnp.array(places, jnp.int32)[lax.axis_index(axis)]
    return onward, back, place


def ring_reduce(pick, axis, count):
    onward, back, place = ring_steps(axis, count)
    half = count // 2
    far = pick((place + half) % count)
    rows = far.shape[0] // 2
    up = lax.ppermute(far[:rows], axis, onward)
    down = lax.ppermute(far[rows:], axis, back)
    for step in range(2, half + 1):
        mine_up = pick((place + half - step + 1) % count)
        mine_down = pick((place + count - half + step - 1) % count)
        if step == 2:
            mine_up = jnp.concatenate([mine_up[:rows] + up, mine_up[rows:]], axis=0)
            mine_down = jnp.concatenate([mine_down[:rows], mine_down[rows:] + down], axis=0)
        else:
            mine_up = mine_up + up
            mine_down = mine_down + down
        up = lax.ppermute(mine_up, axis, onward)
        down = lax.ppermute(mine_down, axis, back)
    own = pick(place).astype(F32)
    return (own + up.astype(F32) + down.astype(F32)).astype(BF16)


def ring_gather(own, axis, count, place_chunk, state, zero=0):
    onward, back, place = ring_steps(axis, count)
    half = count // 2
    rows = own.shape[0] // 2
    state = place_chunk(state, own, place, 0)
    up = down = own
    for step in range(1, half):
        up = lax.ppermute(up, axis, onward)
        down = lax.ppermute(down, axis, back)
        state = place_chunk(state, up, (place + count - step) % count, 0)
        state = place_chunk(state, down, (place + step) % count, 0)
    up = lax.ppermute(lax.dynamic_slice_in_dim(up, zero, rows, 0), axis, onward)
    down = lax.ppermute(lax.dynamic_slice_in_dim(down, zero + rows, rows, 0), axis, back)
    return place_chunk(state, jnp.concatenate([up, down], axis=0), (place + half) % count, 0)


def nothing(array):
    value = array.reshape(-1)[0].astype(jnp.int32)
    return jnp.minimum(jnp.abs(value), 0)


def gather_pairs(own, count):
    if count != 4:
        return lax.all_gather(own, "fsdp", axis=0)
    index = lax.axis_index("fsdp")
    across = lax.ppermute(own, "fsdp", [(k, k ^ 2) for k in range(4)])
    first = index < 2
    pair = jnp.stack([jnp.where(first, own, across), jnp.where(first, across, own)])
    other = lax.ppermute(pair, "fsdp", [(k, k ^ 1) for k in range(4)])
    even = index % 2 == 0
    return jnp.stack([jnp.where(even, pair, other), jnp.where(even, other, pair)], axis=1).reshape(
        (4,) + own.shape
    )


def columns_for_rows(weight, count, zero, later):
    rows, columns = weight.shape
    part = columns // count
    if count != 4:
        parts = weight.reshape(rows, count, part).transpose(1, 0, 2)
        return lax.all_to_all(parts, "fsdp", 0, 0).reshape(count * rows, part)
    index = lax.axis_index("fsdp")
    chip, core = index // 2, index % 2
    mine = lax.dynamic_slice_in_dim(weight, chip * 2 * part, 2 * part, 1)
    theirs = lax.dynamic_slice_in_dim(weight, (1 - chip) * 2 * part + zero, 2 * part, 1)
    across = lax.ppermute(theirs, "fsdp", [(k, k ^ 2) for k in range(4)])
    low = chip == 0
    pair = jnp.stack([jnp.where(low, mine, across), jnp.where(low, across, mine)])
    even = core == 0
    other = lax.ppermute(
        lax.dynamic_slice_in_dim(pair, (1 - core) * part + later, part, 2),
        "fsdp",
        [(k, k ^ 1) for k in range(4)],
    )
    kept = lax.dynamic_slice_in_dim(pair, core * part, part, 2)
    return jnp.stack(
        [jnp.where(even, kept, other), jnp.where(even, other, kept)], axis=1
    ).reshape(count * rows, part)


def turn(heads, cosine, sine):
    lane = lax.broadcasted_iota(jnp.int32, heads.shape, 1) % DH
    partner = jnp.where(
        lane < ROT // 2,
        pltpu.roll(heads, PAIR - ROT // 2, 1),
        pltpu.roll(heads, ROT // 2, 1),
    )
    return heads * cosine + partner * sine


def project_kernel(tokens_ref, upstream_ref, params_ref, weight_ref, bias_ref, dense_ref, cos_ref,
                   sin_ref, out_ref, attn_ref, ff_ref, normed_ref):
    @pl.when(pl.program_id(1) == 0)
    def norm():
        inputs = tokens_ref[0, 0].astype(F32)
        centered = inputs - jnp.mean(inputs, axis=-1, keepdims=True)
        variance = jnp.mean(centered * centered, axis=-1, keepdims=True)
        normed = centered * lax.rsqrt(variance + EPSILON)
        normed_ref[...] = normed.astype(BF16)
        attn_ref[...] = (normed * params_ref[0:1] + params_ref[1:2]).astype(BF16)
        ff_ref[...] = (normed * params_ref[2:3] + params_ref[3:4]).astype(BF16)

    joint = dot(attn_ref[...], weight_ref[...]) + bias_ref[...].astype(F32)
    low = lax.broadcasted_iota(jnp.int32, (joint.shape[0], PAIR), 1) < DH
    one, two, three = joint[:, :PAIR], joint[:, PAIR : 2 * PAIR], joint[:, 2 * PAIR :]
    query = jnp.where(low, one, two)
    key = pltpu.roll(jnp.where(low, three, one), DH, 1)
    value = jnp.where(low, two, three)
    cosine, sine = cos_ref[...], sin_ref[...]
    out_ref[0, :, :PAIR] = turn(query, cosine, sine).astype(BF16)
    out_ref[0, :, PAIR : 2 * PAIR] = turn(key, cosine, sine).astype(BF16)
    out_ref[0, :, 2 * PAIR : 3 * PAIR] = value.astype(BF16)
    out_ref[0, :, 3 * PAIR :] = dot(upstream_ref[0, 0], dense_ref[...], 1, 1).astype(BF16)


def project(both, params, weight, bias, dense, cosine, sine, seqs, tokens, pairs):
    wide = jax.ShapeDtypeStruct((seqs * tokens, D), BF16)
    rows = pl.BlockSpec((tokens, D), lambda s, p: (s, 0))
    return pl.pallas_call(
        project_kernel,
        grid=(seqs, pairs),
        in_specs=[
            pl.BlockSpec((1, 1, tokens, D), lambda s, p: (s, 0, 0, 0)),
            pl.BlockSpec((1, 1, tokens, D), lambda s, p: (s, 1, 0, 0)),
            pl.BlockSpec((4, D), lambda s, p: (0, 0)),
            pl.BlockSpec((D, 3 * PAIR), lambda s, p: (0, p)),
            pl.BlockSpec((1, 3 * PAIR), lambda s, p: (0, p)),
            pl.BlockSpec((PAIR, D), lambda s, p: (p, 0)),
            pl.BlockSpec((tokens, PAIR), lambda s, p: (s, 0)),
            pl.BlockSpec((tokens, PAIR), lambda s, p: (s, 0)),
        ],
        out_specs=[
            pl.BlockSpec((1, tokens, 4 * PAIR), lambda s, p: (s * pairs + p, 0, 0)),
            rows,
            rows,
            rows,
        ],
        out_shape=[
            jax.ShapeDtypeStruct((seqs * pairs, tokens, 4 * PAIR), BF16), wide, wide, wide,
        ],
        compiler_params=pltpu.CompilerParams(vmem_limit_bytes=40 * MIB),
        cost_estimate=pl.CostEstimate(
            flops=3 * seqs * pairs * tokens * D * 4 * PAIR,
            bytes_accessed=16 * MIB,
            transcendentals=0,
        ),
        name="project",
    )(both, both, params, weight, bias, dense, cosine, sine)


def unturn_kernel(back_ref, cos_ref, sin_ref, first_ref, grad_ref, mixed_ref):
    cosine, sine = cos_ref[...], sin_ref[...]
    query = turn(back_ref[0, :, PAIR : 2 * PAIR].astype(F32), cosine, -sine)
    key = turn(back_ref[0, :, 2 * PAIR : 3 * PAIR].astype(F32), cosine, -sine)
    value = back_ref[0, :, 3 * PAIR :].astype(F32)
    low = lax.broadcasted_iota(jnp.int32, query.shape, 1) < DH
    key = pltpu.roll(key, DH, 1)
    grad_ref[:, :PAIR] = jnp.where(low, query, key).astype(BF16)
    grad_ref[:, PAIR : 2 * PAIR] = jnp.where(low, value, query).astype(BF16)
    grad_ref[:, 2 * PAIR :] = jnp.where(low, key, value).astype(BF16)
    mixed_ref[...] = back_ref[0, :, :PAIR]


def unturn(back, cosine, sine, first, seqs, tokens, pairs):
    return pl.pallas_call(
        unturn_kernel,
        grid=(seqs, pairs),
        in_specs=[
            pl.BlockSpec((1, tokens, 4 * PAIR), lambda s, p: (s * pairs + p, 0, 0)),
            pl.BlockSpec((tokens, PAIR), lambda s, p: (s, 0)),
            pl.BlockSpec((tokens, PAIR), lambda s, p: (s, 0)),
            pl.BlockSpec(memory_space=pl.ANY),
        ],
        out_specs=[
            pl.BlockSpec((tokens, 3 * PAIR), lambda s, p: (s, p)),
            pl.BlockSpec((tokens, PAIR), lambda s, p: (s, p)),
        ],
        out_shape=[
            jax.ShapeDtypeStruct((seqs * tokens, pairs * 3 * PAIR), BF16),
            jax.ShapeDtypeStruct((seqs * tokens, pairs * PAIR), BF16),
        ],
        compiler_params=pltpu.CompilerParams(vmem_limit_bytes=32 * MIB),
        cost_estimate=pl.CostEstimate(flops=8 * MIB, bytes_accessed=5 * MIB, transcendentals=0),
        name="unturn",
    )(back, cosine, sine, first)


def attend_kernel(tile, block, unrolled, order_ref, in_ref, first_ref, out_ref, sorted_ref, flipped_ref,
                  score_ref, prob_ref, mixed_ref, dq_ref, dk_ref, dv_ref):
    head = pl.program_id(0)
    length = in_ref.shape[0]
    tiles = length // tile
    blocks = length // block

    def loop(count, body, carry):
        if unrolled:
            for index in range(count):
                carry = body(index, carry)
            return carry
        return lax.fori_loop(0, count, body, carry)

    def span(index, size):
        start = index * size
        if not isinstance(start, int):
            start = pl.multiple_of(start, size)
        return pl.ds(start, size)

    @pl.when(head == 0)
    def prepare():
        def one(index, carry):
            sorted_ref[span(order_ref[index], block), :] = in_ref[span(index, block), :]
            return carry

        loop(blocks, one, 0)

        def flip(index, carry):
            flipped_ref[:, span(index, tile)] = sorted_ref[span(index, tile), :].T
            return carry

        loop(tiles, flip, 0)
        dk_ref[...] = jnp.zeros_like(dk_ref)
        dv_ref[...] = jnp.zeros_like(dv_ref)

    first = pl.multiple_of(head * DH, DH)

    def padded(rows):
        rows = rows.astype(F32)
        zero = jnp.zeros_like(rows)
        upper = jnp.where(head == 0, rows, zero)
        lower = jnp.where(head == 0, zero, rows)
        return jnp.concatenate([upper, lower], axis=0).astype(BF16)

    def one_tile(i, carry):
        query = padded(flipped_ref[pl.ds(first, DH), span(i, tile)])

        def score(j, top):
            part = dot(sorted_ref[span(j, tile), PAIR : 2 * PAIR], query)
            if not (unrolled and j < i):
                keys = j * tile + lax.broadcasted_iota(jnp.int32, part.shape, 0)
                queries = i * tile + lax.broadcasted_iota(jnp.int32, part.shape, 1)
                part = jnp.where(keys <= queries, part, MASKED)
            score_ref[span(j, tile), :] = part
            return jnp.maximum(top, jnp.max(part, axis=0, keepdims=True))

        top = loop(i + 1, score, jnp.full((1, tile), -3e38, F32))
        shift = top * (SCALE * LOG2E)

        def mix(j, status):
            total, mixed = status
            prob = jnp.exp2(score_ref[span(j, tile), :] * (SCALE * LOG2E) - shift)
            low = prob.astype(BF16)
            prob_ref[span(j, tile), :] = low
            total = total + jnp.sum(prob, axis=0, keepdims=True)
            values = flipped_ref[pl.ds(2 * PAIR + first, DH), span(j, tile)]
            return total, mixed + dot(values, low)

        total, mixed = loop(
            i + 1, mix, (jnp.zeros((1, tile), F32), jnp.zeros((DH, tile), F32))
        )
        inverse = 1.0 / total
        mixed = mixed * inverse
        mixed_ref[pl.ds(first, DH), span(i, tile)] = mixed
        grad = flipped_ref[pl.ds(3 * PAIR + first, DH), span(i, tile)].astype(F32) * inverse
        grad = grad.astype(BF16)
        delta = jnp.sum(grad.astype(F32) * mixed, axis=0, keepdims=True)
        grad = padded(grad)

        def pull(j, dq):
            low = prob_ref[span(j, tile), :]
            prob_grad = dot(sorted_ref[span(j, tile), 2 * PAIR : 3 * PAIR], grad)
            score_grad = (low.astype(F32) * (prob_grad - delta)).astype(BF16)
            dv_ref[span(j, tile), :] += dot(low, grad, 1, 1)
            dk_ref[span(j, tile), :] += dot(score_grad, query, 1, 1)
            keys = flipped_ref[pl.ds(PAIR + first, DH), span(j, tile)]
            return dq + dot(keys, score_grad)

        dq_ref[pl.ds(first, DH), span(i, tile)] = loop(i + 1, pull, jnp.zeros((DH, tile), F32))
        return carry

    loop(tiles, one_tile, 0)

    @pl.when(head == pl.num_programs(0) - 1)
    def finish():
        def one(index, carry):
            source = span(order_ref[index], block)
            target = span(index, block)
            out_ref[target, :PAIR] = mixed_ref[:, source].T.astype(BF16)
            out_ref[target, PAIR : 2 * PAIR] = (dq_ref[:, source].T * SCALE).astype(BF16)
            out_ref[target, 2 * PAIR : 3 * PAIR] = (dk_ref[source, :] * SCALE).astype(BF16)
            out_ref[target, 3 * PAIR :] = dv_ref[source, :].astype(BF16)
            return carry

        loop(blocks, one, 0)


def attend(order, packed, block, first):
    length = packed.shape[0]
    unrolled = length <= 2048
    tile = 256 if unrolled else 128
    return pl.pallas_call(
        functools.partial(attend_kernel, tile, block, unrolled),
        grid=(2,),
        in_specs=[
            pl.BlockSpec(memory_space=pltpu.SMEM),
            pl.BlockSpec(memory_space=pltpu.VMEM),
            pl.BlockSpec(memory_space=pl.ANY),
        ],
        out_specs=pl.BlockSpec(memory_space=pltpu.VMEM),
        out_shape=jax.ShapeDtypeStruct((length, 4 * PAIR), BF16),
        scratch_shapes=[
            pltpu.VMEM((length, 4 * PAIR), BF16),
            pltpu.VMEM((4 * PAIR, length), BF16),
            pltpu.VMEM((length, tile), F32),
            pltpu.VMEM((length, tile), BF16),
            pltpu.VMEM((PAIR, length), F32),
            pltpu.VMEM((PAIR, length), F32),
            pltpu.VMEM((length, PAIR), F32),
            pltpu.VMEM((length, PAIR), F32),
        ],
        compiler_params=pltpu.CompilerParams(
            vmem_limit_bytes=(40 if unrolled else 60) * MIB,
            dimension_semantics=("arbitrary",),
        ),
        cost_estimate=pl.CostEstimate(
            flops=56 * length * length * PAIR, bytes_accessed=4 * MIB, transcendentals=0
        ),
        name="attend",
    )(order, packed, first)


def feed_kernel(hidden_ref, inner_ref, bias_ref, outer_ref, upstream_ref,
                outer_grad_ref, inner_grad_ref, bias_grad_ref, out_ref, hidden_grad_ref):
    step = pl.program_id(0)
    hidden, upstream = hidden_ref[...], upstream_ref[...]
    inner = dot(hidden, inner_ref[...]) + bias_ref[...].astype(F32)
    share = 0.5 + 0.5 * lax.erf(inner * (0.5 ** 0.5))
    density = jnp.exp(inner * inner * -0.5) * (1.0 / math.sqrt(2.0 * math.pi))
    activated = (inner * share).astype(BF16)
    slope = share + inner * density
    inner_grad = (dot(upstream, outer_ref[...], 1, 1) * slope).astype(BF16)
    outer_grad_ref[...] = dot(activated, upstream, 0, 0).astype(BF16)
    inner_grad_ref[...] = dot(hidden, inner_grad, 0, 0).astype(BF16)
    bias_grad_ref[...] = jnp.sum(inner_grad.astype(F32), axis=0, keepdims=True)
    out = dot(activated, outer_ref[...])
    hidden_grad = dot(inner_grad, inner_ref[...], 1, 1)

    @pl.when(step == 0)
    def begin():
        out_ref[...] = out
        hidden_grad_ref[...] = hidden_grad

    @pl.when(step > 0)
    def add():
        out_ref[...] += out
        hidden_grad_ref[...] += hidden_grad


def feed(hidden, inner, bias, outer, upstream):
    tokens, columns = hidden.shape[0], inner.shape[1]
    tile = 256
    whole = pl.BlockSpec((tokens, D), lambda t: (0, 0))
    return pl.pallas_call(
        feed_kernel,
        grid=(columns // tile,),
        in_specs=[
            whole,
            pl.BlockSpec((D, tile), lambda t: (0, t)),
            pl.BlockSpec((1, tile), lambda t: (0, t)),
            pl.BlockSpec((tile, D), lambda t: (t, 0)),
            whole,
        ],
        out_specs=[
            pl.BlockSpec((tile, D), lambda t: (t, 0)),
            pl.BlockSpec((D, tile), lambda t: (0, t)),
            pl.BlockSpec((1, tile), lambda t: (0, t)),
            whole,
            whole,
        ],
        out_shape=[
            jax.ShapeDtypeStruct((columns, D), BF16),
            jax.ShapeDtypeStruct((D, columns), BF16),
            jax.ShapeDtypeStruct((1, columns), F32),
            jax.ShapeDtypeStruct((tokens, D), F32),
            jax.ShapeDtypeStruct((tokens, D), F32),
        ],
        compiler_params=pltpu.CompilerParams(vmem_limit_bytes=48 * MIB),
        cost_estimate=pl.CostEstimate(
            flops=0, bytes_accessed=0, transcendentals=0
        ),
        name="feed",
    )(hidden, inner, bias, outer, upstream)


def unpack_kernel(outer_rows, parts, in_ref, outer_ref, inner_ref):
    per = inner_ref.shape[0]
    width = in_ref.shape[2]
    outer_ref[...] = in_ref[0, :outer_rows].astype(F32)
    for part in range(parts):
        start = outer_rows + part * per
        inner_ref[:, part * width : (part + 1) * width] = in_ref[0, start : start + per].astype(F32)


def unpack(packed, outer_rows, parts):
    count, rows, width = packed.shape
    per = (rows - outer_rows) // parts
    if per % 16:
        outer = packed[:, :outer_rows].reshape(-1, width).astype(F32)
        inner = packed[:, outer_rows:].reshape(count, parts, per, width).transpose(0, 2, 1, 3)
        return outer, inner.reshape(count * per, -1).astype(F32)
    return pl.pallas_call(
        functools.partial(unpack_kernel, outer_rows, parts),
        grid=(count,),
        in_specs=[pl.BlockSpec((1, rows, width), lambda c: (c, 0, 0))],
        out_specs=[
            pl.BlockSpec((outer_rows, width), lambda c: (c, 0)),
            pl.BlockSpec((per, parts * width), lambda c: (c, 0)),
        ],
        out_shape=[
            jax.ShapeDtypeStruct((count * outer_rows, width), F32),
            jax.ShapeDtypeStruct((count * per, parts * width), F32),
        ],
        compiler_params=pltpu.CompilerParams(vmem_limit_bytes=16 * MIB),
        cost_estimate=pl.CostEstimate(flops=0, bytes_accessed=13 * MIB, transcendentals=0),
        name="unpack",
    )(packed)


def lay_out_kernel(parts, blocks, per, numbers_ref, *refs):
    count = len(refs) - 3
    joint_ref, dense_ref, vectors_ref = refs[count:]
    lanes = vectors_ref.shape[1]
    columns = parts * blocks
    for k in range(count):
        chunk_ref = refs[k]
        rows = pl.ds(pl.multiple_of(numbers_ref[k] * per, per), per)
        for c in range(columns):
            joint_ref[rows, c * lanes : (c + 1) * lanes] = chunk_ref[c * per : (c + 1) * per].astype(F32)
        first = columns * per
        for c in range(dense_ref.shape[1] // lanes):
            start = first + c * per
            dense_ref[rows, c * lanes : (c + 1) * lanes] = chunk_ref[start : start + per].astype(F32)
        first += dense_ref.shape[1] // lanes * per
        rows = pl.ds(pl.multiple_of(numbers_ref[k] * 16, 16), 16)
        vectors_ref[rows, :] = chunk_ref[first : first + 16].astype(F32)


def lay_out(numbers, chunks, parts, blocks, per, joint_shape, dense_shape):
    lanes = chunks[0].shape[1]
    whole = pl.BlockSpec(memory_space=pltpu.VMEM)
    return pl.pallas_call(
        functools.partial(lay_out_kernel, parts, blocks, per),
        in_specs=[pl.BlockSpec(memory_space=pltpu.SMEM)] + [whole] * len(chunks),
        out_specs=[whole] * 3,
        out_shape=[
            jax.ShapeDtypeStruct(joint_shape, F32),
            jax.ShapeDtypeStruct(dense_shape, F32),
            jax.ShapeDtypeStruct((16 * len(chunks), lanes), F32),
        ],
        compiler_params=pltpu.CompilerParams(vmem_limit_bytes=24 * MIB),
        cost_estimate=pl.CostEstimate(flops=0, bytes_accessed=6 * MIB, transcendentals=0),
        name="lay_out",
    )(numbers, *chunks)


def spread_out(part, ctx, each):
    if ctx > part.shape[0]:
        part = jnp.concatenate([part] * (ctx // part.shape[0]), axis=0)
    return lax.all_to_all(part.reshape((ctx, each) + part.shape[1:]), "ctx", 0, 0)


def rotary_tables(token_pos):
    lane = jnp.arange(PAIR, dtype=jnp.int32) % DH
    exponent = (2 * (lane % (ROT // 2))).astype(F32) / ROT
    inverse = 10000.0 ** (-exponent)
    phases = token_pos[:, None] * inverse[None, :]
    turned = (lane < ROT)[None, :]
    sign = jnp.where(lane < ROT // 2, -1.0, 1.0)[None, :]
    return jnp.where(turned, jnp.cos(phases), 1.0), jnp.where(turned, jnp.sin(phases) * sign, 0.0)


def per_device(ctx, fsdp, tokens, cotangent, positions, block_order, joint_weight, joint_bias,
               dense_weight, dense_bias, inner_weight, inner_bias, outer_weight, outer_bias,
               attention_gain, attention_shift, feedforward_gain, feedforward_shift):
    seqs = fsdp
    count = tokens.shape[1]
    block = count // 2
    rows = joint_weight.shape[0]
    heads = H // fsdp
    pairs = heads // 2
    joint_cols = heads * 3 * DH
    inner_cols = inner_weight.shape[1] // fsdp
    all_tokens = seqs * count
    me = lax.axis_index("ctx")

    pos = positions[0]
    table = block_order[0].astype(BF16)
    extra = jnp.stack(
        [
            attention_gain, attention_shift, feedforward_gain, feedforward_shift,
            dense_bias, outer_bias, (pos // 128).astype(BF16), (pos % 128).astype(BF16),
            jnp.pad(table, (0, rows - table.shape[0])),
        ]
    )
    extra = gather_pairs(jnp.pad(extra, ((0, 7), (0, 0))), fsdp).astype(F32)
    both = gather_pairs(jnp.concatenate([tokens, cotangent], axis=0), fsdp)
    joint_local = lax.all_to_all(
        joint_weight.reshape(rows, fsdp, joint_cols).transpose(1, 0, 2), "fsdp", 0, 0
    ).reshape(D, joint_cols)
    upstream = both[:, 1].reshape(all_tokens, D)

    params = extra[:, :4].transpose(1, 0, 2).reshape(4, D)
    bias_sum = (extra[:, 4] + extra[:, 5]).reshape(D)
    token_pos = (extra[:, 6] * 128.0 + extra[:, 7]).reshape(all_tokens)
    tables = extra[:, 8, : table.shape[0]].astype(jnp.int32)

    cosine, sine = rotary_tables(token_pos)

    sent, hidden_attn, hidden_ff, normed = project(
        both, params, joint_local, joint_bias[None], dense_weight, cosine, sine, seqs, count, pairs
    )
    jobs = seqs * pairs
    each = max(1, jobs // ctx)
    got = spread_out(sent, ctx, each)
    backs = []
    for k in range(each):
        sequence = (lax.rem(me, jobs) * each + k) // pairs
        order = lax.dynamic_index_in_dim(tables, sequence, 0, keepdims=False)
        out = attend(order, got[:, k].reshape(ctx * count, 4 * PAIR), block, sent)
        backs.append(out.reshape(ctx, count, 4 * PAIR))
    back = backs[0][:, None] if each == 1 else jnp.stack(backs, axis=1)
    inner_local = columns_for_rows(inner_weight, fsdp, nothing(got), nothing(back))

    outer_weight_grad, inner_weight_grad, inner_bias_grad, ff_out, hidden_ff_grad = feed(
        hidden_ff, inner_local, inner_bias[None], outer_weight, upstream
    )
    inner_bias_grad = inner_bias_grad[0]

    per = rows // ctx
    outer_rows = outer_weight.shape[0] // ctx
    inner_terms = inner_weight_grad.reshape(fsdp, ctx, per, inner_cols).transpose(1, 0, 2, 3)
    ff_terms = jnp.concatenate(
        [
            outer_weight_grad.reshape(ctx, outer_rows, D),
            inner_terms.reshape(ctx, fsdp * per, inner_cols),
        ],
        axis=1,
    )
    ff_own = lax.psum_scatter(ff_terms, "ctx", scatter_dimension=0)
    back = lax.all_to_all(back, "ctx", 0, 0)[: jobs // each].reshape(jobs, count, 4 * PAIR)
    joint_grad, mixed = unturn(back, cosine, sine, ff_terms, seqs, count, pairs)

    out_part = (ff_out + dot(mixed, dense_weight)).astype(BF16)
    hidden_attn_grad = dot(joint_grad, joint_local, 1, 1)
    e_part = (params[0] * hidden_attn_grad + params[2] * hidden_ff_grad).astype(BF16)
    parts = lax.all_to_all(
        jnp.concatenate([out_part.reshape(seqs, count, D), e_part.reshape(seqs, count, D)], axis=1),
        "fsdp", 0, 0,
    )

    dense_weight_grad = dot(mixed, upstream, 0, 0).astype(BF16)
    joint_weight_grad = dot(hidden_attn, joint_grad, 0, 0).astype(BF16)
    joint_bias_grad = jnp.sum(joint_grad.astype(F32), axis=0)
    upstream_grad = jnp.sum(upstream.astype(F32), axis=0)

    gains = jnp.stack(
        [
            jnp.sum(hidden_attn_grad * normed.astype(F32), axis=0),
            jnp.sum(hidden_attn_grad, axis=0),
            jnp.sum(hidden_ff_grad * normed.astype(F32), axis=0),
            jnp.sum(hidden_ff_grad, axis=0),
        ]
    ).astype(BF16)
    lanes = 2 * PAIR
    gains = gains.reshape(4, fsdp, ctx, per).transpose(2, 1, 0, 3).reshape(ctx, fsdp, 4 * per)
    gains = jnp.pad(gains, ((0, 0), (0, 0), (0, lanes - 4 * per)))
    my_rows = lax.dynamic_slice_in_dim(
        upstream_grad, lax.axis_index("fsdp") * rows, rows, 0
    )
    small = jnp.concatenate(
        [joint_bias_grad.reshape(ctx, -1), inner_bias_grad.reshape(ctx, -1), my_rows.reshape(ctx, -1)],
        axis=1,
    ).astype(BF16)
    small = jnp.pad(small[:, None], ((0, 0), (0, 31 - fsdp), (0, lanes - small.shape[1])))
    joint_blocks, dense_blocks = joint_cols // lanes, D // lanes
    terms = jnp.concatenate(
        [
            joint_weight_grad.reshape(fsdp, ctx, per, joint_blocks, lanes)
            .transpose(1, 0, 3, 2, 4).reshape(ctx, -1, lanes),
            dense_weight_grad.reshape(ctx, per, dense_blocks, lanes)
            .transpose(0, 2, 1, 3).reshape(ctx, -1, lanes),
            gains,
            small,
        ],
        axis=1,
    )
    own = ring_reduce(lambda k: lax.dynamic_index_in_dim(terms, k, 0, keepdims=False), "ctx", ctx)
    joint_rows = fsdp * joint_blocks * per
    dense_rows = dense_blocks * per
    ahead = joint_rows + dense_rows
    gain_rows = jnp.pad(own[ahead : ahead + fsdp][:, None], ((0, 0), (0, 15), (0, 0)))
    joint_part = lax.dynamic_slice_in_dim(own, nothing(parts), joint_rows, 0)
    late_rows = joint_blocks * per + 16
    exchanged = jnp.concatenate(
        [
            joint_part.reshape(fsdp, joint_blocks * per, lanes),
            gain_rows,
            ff_own[outer_rows:].reshape(fsdp, per, -1, lanes).transpose(0, 2, 1, 3).reshape(
                fsdp, -1, lanes
            ),
        ],
        axis=1,
    )
    exchanged = lax.all_to_all(exchanged, "fsdp", 0, 0)
    inner_own = exchanged[:, late_rows:].reshape(fsdp, -1, per, lanes).transpose(0, 2, 1, 3)
    ff_own = jnp.concatenate(
        [ff_own[:outer_rows], inner_own.reshape(fsdp * per, inner_cols)], axis=0
    )
    ff_all = lax.all_gather(ff_own, "ctx", axis=0)
    outer_total, inner_total = unpack(ff_all, outer_rows, fsdp)
    gain_own = jnp.sum(exchanged[:, joint_blocks * per].astype(F32), axis=0).astype(BF16)
    own = jnp.concatenate(
        [
            exchanged[:, : joint_blocks * per].reshape(joint_rows, lanes),
            own[joint_rows:ahead],
            jnp.pad(gain_own[None], ((0, fsdp - 1), (0, 0))),
            own[ahead + fsdp :],
        ],
        axis=0,
    )

    def place_late(state, chunk, number, part):
        joint_state, dense_state, vectors = state
        wide = chunk[:joint_rows].reshape(fsdp, joint_blocks, per, lanes).transpose(2, 0, 1, 3)
        joint_state = lax.dynamic_update_slice_in_dim(
            joint_state, wide.reshape(per, -1).astype(F32), number * per, 0
        )
        wide = chunk[joint_rows:ahead].reshape(dense_blocks, per, lanes).transpose(1, 0, 2)
        dense_state = lax.dynamic_update_slice_in_dim(
            dense_state, wide.reshape(per, -1).astype(F32), number * per, 0
        )
        pieces = jnp.stack([chunk[ahead + fsdp], chunk[ahead]])[None]
        vectors = lax.dynamic_update_slice_in_dim(vectors, pieces.astype(F32), number, 0)
        return joint_state, dense_state, vectors

    if per % 16:
        joint_total, dense_total, vectors = ring_gather(
            own, "ctx", ctx, place_late,
            (jnp.zeros(joint_weight.shape, F32), jnp.zeros(dense_weight.shape, F32),
             jnp.zeros((ctx, 2, lanes), F32)),
        )
    else:
        chunks, numbers = ring_gather(
            own, "ctx", ctx,
            lambda state, chunk, number, part: (state[0] + [chunk], state[1] + [number]),
            ([], []),
        )
        joint_total, dense_total, vectors = lay_out(
            jnp.stack(numbers).astype(jnp.int32), chunks, fsdp, joint_blocks, per,
            joint_weight.shape, dense_weight.shape,
        )
        vectors = vectors.reshape(ctx, 16, lanes)
        vectors = jnp.stack([vectors[:, fsdp], vectors[:, 0]], axis=1)
    a, b = joint_cols // ctx, inner_cols // ctx
    joint_bias_total = vectors[:, 0, :a].reshape(-1)
    inner_bias_total = vectors[:, 0, a : a + b].reshape(-1)
    upstream_total = vectors[:, 0, a + b : a + b + per].reshape(-1)
    gain_totals = [vectors[:, 1, k * per : (k + 1) * per].reshape(-1) for k in range(4)]

    layer_output = (tokens[0].astype(F32) + bias_sum
                    + jnp.sum(parts[:, :count].astype(F32), axis=0)).astype(BF16)
    e = jnp.sum(parts[:, count:].astype(F32), axis=0)
    mine = tokens[0].astype(F32)
    mine_centered = mine - jnp.mean(mine, axis=-1, keepdims=True)
    mine_spread = lax.rsqrt(jnp.mean(mine_centered * mine_centered, axis=-1, keepdims=True) + EPSILON)
    mine_normed = mine_centered * mine_spread
    tokens_grad = (
        cotangent[0].astype(F32)
        + (e - jnp.mean(e, axis=-1, keepdims=True)
           - mine_normed * jnp.mean(e * mine_normed, axis=-1, keepdims=True)) * mine_spread
    ).astype(BF16)

    return (
        layer_output[None], tokens_grad[None],
        joint_total, joint_bias_total, dense_total, upstream_total,
        inner_total, inner_bias_total, outer_total, upstream_total,
        gain_totals[0], gain_totals[1], gain_totals[2], gain_totals[3],
    )


def solution(mesh):
    tokens = P("fsdp", "ctx", None)
    weight = P("fsdp", None)
    vector = P("fsdp")
    return jax.shard_map(
        functools.partial(per_device, mesh.shape["ctx"], mesh.shape["fsdp"]),
        mesh=mesh,
        in_specs=(tokens, tokens, P("fsdp", "ctx"), weight) + (weight, vector) * 4 + (vector,) * 4,
        out_specs=(tokens, tokens) + (weight, vector) * 4 + (vector,) * 4,
        check_vma=False,
    )
```

```python
import functools
import math

import jax
import jax.numpy as jnp
from jax import lax
from jax.experimental import pallas as pl
from jax.experimental.pallas import tpu as pltpu
from jax.sharding import PartitionSpec as P

D = 1024
H = 16
DH = 64
ROT = 16
PAIR = 2 * DH
EPSILON = 1e-05
MASKED = -1e30
SCALE = DH ** (-0.5)
LOG2E = math.log2(math.e)
BF16 = jnp.bfloat16
F32 = jnp.float32
MIB = 1024 * 1024


def dot(left, right, left_dim=1, right_dim=0):
    return lax.dot_general(
        left, right, (((left_dim,), (right_dim,)), ((), ())), preferred_element_type=F32
    )


def ring_order(count):
    return list(range(0, count, 2)) + list(range(1, count, 2))[::-1]


def ring_steps(axis, count):
    order = ring_order(count)
    onward = [(order[k], order[(k + 1) % count]) for k in range(count)]
    back = [(b, a) for a, b in onward]
    places = [0] * count
    for place, index in enumerate(order):
        places[index] = place
    place = jnp.array(places, jnp.int32)[lax.axis_index(axis)]
    return onward, back, place


def ring_reduce(pick, axis, count):
    onward, back, place = ring_steps(axis, count)
    half = count // 2
    far = pick((place + half) % count)
    rows = far.shape[0] // 2
    up = lax.ppermute(far[:rows], axis, onward)
    down = lax.ppermute(far[rows:], axis, back)
    for step in range(2, half + 1):
        mine_up = pick((place + half - step + 1) % count)
        mine_down = pick((place + count - half + step - 1) % count)
        if step == 2:
            mine_up = jnp.concatenate([mine_up[:rows] + up, mine_up[rows:]], axis=0)
            mine_down = jnp.concatenate([mine_down[:rows], mine_down[rows:] + down], axis=0)
        else:
            mine_up = mine_up + up
            mine_down = mine_down + down
        up = lax.ppermute(mine_up, axis, onward)
        down = lax.ppermute(mine_down, axis, back)
    own = pick(place).astype(F32)
    return (own + up.astype(F32) + down.astype(F32)).astype(BF16)


def ring_gather(own, axis, count, place_chunk, state, zero=0):
    onward, back, place = ring_steps(axis, count)
    half = count // 2
    rows = own.shape[0] // 2
    state = place_chunk(state, own, place, 0)
    up = down = own
    for step in range(1, half):
        up = lax.ppermute(up, axis, onward)
        down = lax.ppermute(down, axis, back)
        state = place_chunk(state, up, (place + count - step) % count, 0)
        state = place_chunk(state, down, (place + step) % count, 0)
    up = lax.ppermute(lax.dynamic_slice_in_dim(up, zero, rows, 0), axis, onward)
    down = lax.ppermute(lax.dynamic_slice_in_dim(down, zero + rows, rows, 0), axis, back)
    return place_chunk(state, jnp.concatenate([up, down], axis=0), (place + half) % count, 0)


def nothing(array):
    value = array.reshape(-1)[0].astype(jnp.int32)
    return jnp.minimum(jnp.abs(value), 0)


def gather_pairs(own, count):
    if count != 4:
        return lax.all_gather(own, "fsdp", axis=0)
    index = lax.axis_index("fsdp")
    across = lax.ppermute(own, "fsdp", [(k, k ^ 2) for k in range(4)])
    first = index < 2
    pair = jnp.stack([jnp.where(first, own, across), jnp.where(first, across, own)])
    other = lax.ppermute(pair, "fsdp", [(k, k ^ 1) for k in range(4)])
    even = index % 2 == 0
    return jnp.stack([jnp.where(even, pair, other), jnp.where(even, other, pair)], axis=1).reshape(
        (4,) + own.shape
    )


def columns_for_rows(weight, count, zero, later):
    rows, columns = weight.shape
    part = columns // count
    if count != 4:
        parts = weight.reshape(rows, count, part).transpose(1, 0, 2)
        return lax.all_to_all(parts, "fsdp", 0, 0).reshape(count * rows, part)
    index = lax.axis_index("fsdp")
    chip, core = index // 2, index % 2
    mine = lax.dynamic_slice_in_dim(weight, chip * 2 * part, 2 * part, 1)
    theirs = lax.dynamic_slice_in_dim(weight, (1 - chip) * 2 * part + zero, 2 * part, 1)
    across = lax.ppermute(theirs, "fsdp", [(k, k ^ 2) for k in range(4)])
    low = chip == 0
    pair = jnp.stack([jnp.where(low, mine, across), jnp.where(low, across, mine)])
    even = core == 0
    other = lax.ppermute(
        lax.dynamic_slice_in_dim(pair, (1 - core) * part + later, part, 2),
        "fsdp",
        [(k, k ^ 1) for k in range(4)],
    )
    kept = lax.dynamic_slice_in_dim(pair, core * part, part, 2)
    return jnp.stack(
        [jnp.where(even, kept, other), jnp.where(even, other, kept)], axis=1
    ).reshape(count * rows, part)


def turn(heads, cosine, sine):
    lane = lax.broadcasted_iota(jnp.int32, heads.shape, 1) % DH
    partner = jnp.where(
        lane < ROT // 2,
        pltpu.roll(heads, PAIR - ROT // 2, 1),
        pltpu.roll(heads, ROT // 2, 1),
    )
    return heads * cosine + partner * sine


def project_kernel(tokens_ref, upstream_ref, params_ref, weight_ref, bias_ref, dense_ref, cos_ref,
                   sin_ref, out_ref, attn_ref, ff_ref, normed_ref):
    @pl.when(pl.program_id(1) == 0)
    def norm():
        inputs = tokens_ref[0, 0].astype(F32)
        centered = inputs - jnp.mean(inputs, axis=-1, keepdims=True)
        variance = jnp.mean(centered * centered, axis=-1, keepdims=True)
        normed = centered * lax.rsqrt(variance + EPSILON)
        normed_ref[...] = normed.astype(BF16)
        attn_ref[...] = (normed * params_ref[0:1] + params_ref[1:2]).astype(BF16)
        ff_ref[...] = (normed * params_ref[2:3] + params_ref[3:4]).astype(BF16)

    joint = dot(attn_ref[...], weight_ref[...]) + bias_ref[...].astype(F32)
    low = lax.broadcasted_iota(jnp.int32, (joint.shape[0], PAIR), 1) < DH
    one, two, three = joint[:, :PAIR], joint[:, PAIR : 2 * PAIR], joint[:, 2 * PAIR :]
    query = jnp.where(low, one, two)
    key = pltpu.roll(jnp.where(low, three, one), DH, 1)
    value = jnp.where(low, two, three)
    cosine, sine = cos_ref[...], sin_ref[...]
    out_ref[0, :, :PAIR] = turn(query, cosine, sine).astype(BF16)
    out_ref[0, :, PAIR : 2 * PAIR] = turn(key, cosine, sine).astype(BF16)
    out_ref[0, :, 2 * PAIR : 3 * PAIR] = value.astype(BF16)
    out_ref[0, :, 3 * PAIR :] = dot(upstream_ref[0, 0], dense_ref[...], 1, 1).astype(BF16)


def project(both, params, weight, bias, dense, cosine, sine, seqs, tokens, pairs):
    wide = jax.ShapeDtypeStruct((seqs * tokens, D), BF16)
    rows = pl.BlockSpec((tokens, D), lambda s, p: (s, 0))
    return pl.pallas_call(
        project_kernel,
        grid=(seqs, pairs),
        in_specs=[
            pl.BlockSpec((1, 1, tokens, D), lambda s, p: (s, 0, 0, 0)),
            pl.BlockSpec((1, 1, tokens, D), lambda s, p: (s, 1, 0, 0)),
            pl.BlockSpec((4, D), lambda s, p: (0, 0)),
            pl.BlockSpec((D, 3 * PAIR), lambda s, p: (0, p)),
            pl.BlockSpec((1, 3 * PAIR), lambda s, p: (0, p)),
            pl.BlockSpec((PAIR, D), lambda s, p: (p, 0)),
            pl.BlockSpec((tokens, PAIR), lambda s, p: (s, 0)),
            pl.BlockSpec((tokens, PAIR), lambda s, p: (s, 0)),
        ],
        out_specs=[
            pl.BlockSpec((1, tokens, 4 * PAIR), lambda s, p: (s * pairs + p, 0, 0)),
            rows,
            rows,
            rows,
        ],
        out_shape=[
            jax.ShapeDtypeStruct((seqs * pairs, tokens, 4 * PAIR), BF16), wide, wide, wide,
        ],
        compiler_params=pltpu.CompilerParams(vmem_limit_bytes=40 * MIB),
        cost_estimate=pl.CostEstimate(
            flops=3 * seqs * pairs * tokens * D * 4 * PAIR,
            bytes_accessed=16 * MIB,
            transcendentals=0,
        ),
        name="project",
    )(both, both, params, weight, bias, dense, cosine, sine)


def unturn_kernel(back_ref, cos_ref, sin_ref, first_ref, grad_ref, mixed_ref):
    cosine, sine = cos_ref[...], sin_ref[...]
    query = turn(back_ref[0, :, PAIR : 2 * PAIR].astype(F32), cosine, -sine)
    key = turn(back_ref[0, :, 2 * PAIR : 3 * PAIR].astype(F32), cosine, -sine)
    value = back_ref[0, :, 3 * PAIR :].astype(F32)
    low = lax.broadcasted_iota(jnp.int32, query.shape, 1) < DH
    key = pltpu.roll(key, DH, 1)
    grad_ref[:, :PAIR] = jnp.where(low, query, key).astype(BF16)
    grad_ref[:, PAIR : 2 * PAIR] = jnp.where(low, value, query).astype(BF16)
    grad_ref[:, 2 * PAIR :] = jnp.where(low, key, value).astype(BF16)
    mixed_ref[...] = back_ref[0, :, :PAIR]


def unturn(back, cosine, sine, first, seqs, tokens, pairs):
    return pl.pallas_call(
        unturn_kernel,
        grid=(seqs, pairs),
        in_specs=[
            pl.BlockSpec((1, tokens, 4 * PAIR), lambda s, p: (s * pairs + p, 0, 0)),
            pl.BlockSpec((tokens, PAIR), lambda s, p: (s, 0)),
            pl.BlockSpec((tokens, PAIR), lambda s, p: (s, 0)),
            pl.BlockSpec(memory_space=pl.ANY),
        ],
        out_specs=[
            pl.BlockSpec((tokens, 3 * PAIR), lambda s, p: (s, p)),
            pl.BlockSpec((tokens, PAIR), lambda s, p: (s, p)),
        ],
        out_shape=[
            jax.ShapeDtypeStruct((seqs * tokens, pairs * 3 * PAIR), BF16),
            jax.ShapeDtypeStruct((seqs * tokens, pairs * PAIR), BF16),
        ],
        compiler_params=pltpu.CompilerParams(vmem_limit_bytes=32 * MIB),
        cost_estimate=pl.CostEstimate(flops=8 * MIB, bytes_accessed=5 * MIB, transcendentals=0),
        name="unturn",
    )(back, cosine, sine, first)


def attend_kernel(tile, block, unrolled, order_ref, in_ref, first_ref, out_ref, sorted_ref, flipped_ref,
                  score_ref, prob_ref, mixed_ref, dq_ref, dk_ref, dv_ref):
    head = pl.program_id(0)
    length = in_ref.shape[0]
    tiles = length // tile
    blocks = length // block

    def loop(count, body, carry):
        if unrolled:
            for index in range(count):
                carry = body(index, carry)
            return carry
        return lax.fori_loop(0, count, body, carry)

    def span(index, size):
        start = index * size
        if not isinstance(start, int):
            start = pl.multiple_of(start, size)
        return pl.ds(start, size)

    @pl.when(head == 0)
    def prepare():
        def one(index, carry):
            sorted_ref[span(order_ref[index], block), :] = in_ref[span(index, block), :]
            return carry

        loop(blocks, one, 0)

        def flip(index, carry):
            flipped_ref[:, span(index, tile)] = sorted_ref[span(index, tile), :].T
            return carry

        loop(tiles, flip, 0)
        dk_ref[...] = jnp.zeros_like(dk_ref)
        dv_ref[...] = jnp.zeros_like(dv_ref)

    first = pl.multiple_of(head * DH, DH)

    def padded(rows):
        rows = rows.astype(F32)
        zero = jnp.zeros_like(rows)
        upper = jnp.where(head == 0, rows, zero)
        lower = jnp.where(head == 0, zero, rows)
        return jnp.concatenate([upper, lower], axis=0).astype(BF16)

    def one_tile(i, carry):
        query = padded(flipped_ref[pl.ds(first, DH), span(i, tile)])

        def score(j, top):
            part = dot(sorted_ref[span(j, tile), PAIR : 2 * PAIR], query)
            if not (unrolled and j < i):
                keys = j * tile + lax.broadcasted_iota(jnp.int32, part.shape, 0)
                queries = i * tile + lax.broadcasted_iota(jnp.int32, part.shape, 1)
                part = jnp.where(keys <= queries, part, MASKED)
            score_ref[span(j, tile), :] = part
            return jnp.maximum(top, jnp.max(part, axis=0, keepdims=True))

        top = loop(i + 1, score, jnp.full((1, tile), -3e38, F32))
        shift = top * (SCALE * LOG2E)

        def mix(j, status):
            total, mixed = status
            prob = jnp.exp2(score_ref[span(j, tile), :] * (SCALE * LOG2E) - shift)
            low = prob.astype(BF16)
            prob_ref[span(j, tile), :] = low
            total = total + jnp.sum(prob, axis=0, keepdims=True)
            values = flipped_ref[pl.ds(2 * PAIR + first, DH), span(j, tile)]
            return total, mixed + dot(values, low)

        total, mixed = loop(
            i + 1, mix, (jnp.zeros((1, tile), F32), jnp.zeros((DH, tile), F32))
        )
        inverse = 1.0 / total
        mixed = mixed * inverse
        mixed_ref[pl.ds(first, DH), span(i, tile)] = mixed
        grad = flipped_ref[pl.ds(3 * PAIR + first, DH), span(i, tile)].astype(F32) * inverse
        grad = grad.astype(BF16)
        delta = jnp.sum(grad.astype(F32) * mixed, axis=0, keepdims=True)
        grad = padded(grad)

        def pull(j, dq):
            low = prob_ref[span(j, tile), :]
            prob_grad = dot(sorted_ref[span(j, tile), 2 * PAIR : 3 * PAIR], grad)
            score_grad = (low.astype(F32) * (prob_grad - delta)).astype(BF16)
            dv_ref[span(j, tile), :] += dot(low, grad, 1, 1)
            dk_ref[span(j, tile), :] += dot(score_grad, query, 1, 1)
            keys = flipped_ref[pl.ds(PAIR + first, DH), span(j, tile)]
            return dq + dot(keys, score_grad)

        dq_ref[pl.ds(first, DH), span(i, tile)] = loop(i + 1, pull, jnp.zeros((DH, tile), F32))
        return carry

    loop(tiles, one_tile, 0)

    @pl.when(head == pl.num_programs(0) - 1)
    def finish():
        def one(index, carry):
            source = span(order_ref[index], block)
            target = span(index, block)
            out_ref[target, :PAIR] = mixed_ref[:, source].T.astype(BF16)
            out_ref[target, PAIR : 2 * PAIR] = (dq_ref[:, source].T * SCALE).astype(BF16)
            out_ref[target, 2 * PAIR : 3 * PAIR] = (dk_ref[source, :] * SCALE).astype(BF16)
            out_ref[target, 3 * PAIR :] = dv_ref[source, :].astype(BF16)
            return carry

        loop(blocks, one, 0)


def attend(order, packed, block, first):
    length = packed.shape[0]
    unrolled = length <= 2048
    tile = 256 if unrolled else 128
    return pl.pallas_call(
        functools.partial(attend_kernel, tile, block, unrolled),
        grid=(2,),
        in_specs=[
            pl.BlockSpec(memory_space=pltpu.SMEM),
            pl.BlockSpec(memory_space=pltpu.VMEM),
            pl.BlockSpec(memory_space=pl.ANY),
        ],
        out_specs=pl.BlockSpec(memory_space=pltpu.VMEM),
        out_shape=jax.ShapeDtypeStruct((length, 4 * PAIR), BF16),
        scratch_shapes=[
            pltpu.VMEM((length, 4 * PAIR), BF16),
            pltpu.VMEM((4 * PAIR, length), BF16),
            pltpu.VMEM((length, tile), F32),
            pltpu.VMEM((length, tile), BF16),
            pltpu.VMEM((PAIR, length), F32),
            pltpu.VMEM((PAIR, length), F32),
            pltpu.VMEM((length, PAIR), F32),
            pltpu.VMEM((length, PAIR), F32),
        ],
        compiler_params=pltpu.CompilerParams(
            vmem_limit_bytes=(40 if unrolled else 60) * MIB,
            dimension_semantics=("arbitrary",),
        ),
        cost_estimate=pl.CostEstimate(
            flops=56 * length * length * PAIR, bytes_accessed=4 * MIB, transcendentals=0
        ),
        name="attend",
    )(order, packed, first)


def feed_kernel(hidden_ref, inner_ref, bias_ref, outer_ref, upstream_ref,
                outer_grad_ref, inner_grad_ref, bias_grad_ref, out_ref, hidden_grad_ref):
    step = pl.program_id(0)
    hidden, upstream = hidden_ref[...], upstream_ref[...]
    inner = dot(hidden, inner_ref[...]) + bias_ref[...].astype(F32)
    share = 0.5 + 0.5 * lax.erf(inner * (0.5 ** 0.5))
    density = jnp.exp(inner * inner * -0.5) * (1.0 / math.sqrt(2.0 * math.pi))
    activated = (inner * share).astype(BF16)
    slope = share + inner * density
    inner_grad = (dot(upstream, outer_ref[...], 1, 1) * slope).astype(BF16)
    outer_grad_ref[...] = dot(activated, upstream, 0, 0).astype(BF16)
    inner_grad_ref[...] = dot(hidden, inner_grad, 0, 0).astype(BF16)
    bias_grad_ref[...] = jnp.sum(inner_grad.astype(F32), axis=0, keepdims=True)
    out = dot(activated, outer_ref[...])
    hidden_grad = dot(inner_grad, inner_ref[...], 1, 1)

    @pl.when(step == 0)
    def begin():
        out_ref[...] = out
        hidden_grad_ref[...] = hidden_grad

    @pl.when(step > 0)
    def add():
        out_ref[...] += out
        hidden_grad_ref[...] += hidden_grad


def feed(hidden, inner, bias, outer, upstream):
    tokens, columns = hidden.shape[0], inner.shape[1]
    tile = 256
    whole = pl.BlockSpec((tokens, D), lambda t: (0, 0))
    return pl.pallas_call(
        feed_kernel,
        grid=(columns // tile,),
        in_specs=[
            whole,
            pl.BlockSpec((D, tile), lambda t: (0, t)),
            pl.BlockSpec((1, tile), lambda t: (0, t)),
            pl.BlockSpec((tile, D), lambda t: (t, 0)),
            whole,
        ],
        out_specs=[
            pl.BlockSpec((tile, D), lambda t: (t, 0)),
            pl.BlockSpec((D, tile), lambda t: (0, t)),
            pl.BlockSpec((1, tile), lambda t: (0, t)),
            whole,
            whole,
        ],
        out_shape=[
            jax.ShapeDtypeStruct((columns, D), BF16),
            jax.ShapeDtypeStruct((D, columns), BF16),
            jax.ShapeDtypeStruct((1, columns), F32),
            jax.ShapeDtypeStruct((tokens, D), F32),
            jax.ShapeDtypeStruct((tokens, D), F32),
        ],
        compiler_params=pltpu.CompilerParams(vmem_limit_bytes=48 * MIB),
        cost_estimate=pl.CostEstimate(
            flops=0, bytes_accessed=0, transcendentals=0
        ),
        name="feed",
    )(hidden, inner, bias, outer, upstream)


def unpack_kernel(outer_rows, parts, in_ref, outer_ref, inner_ref):
    per = inner_ref.shape[0]
    width = in_ref.shape[2]
    outer_ref[...] = in_ref[0, :outer_rows].astype(F32)
    for part in range(parts):
        start = outer_rows + part * per
        inner_ref[:, part * width : (part + 1) * width] = in_ref[0, start : start + per].astype(F32)


def unpack(packed, outer_rows, parts):
    count, rows, width = packed.shape
    per = (rows - outer_rows) // parts
    if per % 16:
        outer = packed[:, :outer_rows].reshape(-1, width).astype(F32)
        inner = packed[:, outer_rows:].reshape(count, parts, per, width).transpose(0, 2, 1, 3)
        return outer, inner.reshape(count * per, -1).astype(F32)
    return pl.pallas_call(
        functools.partial(unpack_kernel, outer_rows, parts),
        grid=(count,),
        in_specs=[pl.BlockSpec((1, rows, width), lambda c: (c, 0, 0))],
        out_specs=[
            pl.BlockSpec((outer_rows, width), lambda c: (c, 0)),
            pl.BlockSpec((per, parts * width), lambda c: (c, 0)),
        ],
        out_shape=[
            jax.ShapeDtypeStruct((count * outer_rows, width), F32),
            jax.ShapeDtypeStruct((count * per, parts * width), F32),
        ],
        compiler_params=pltpu.CompilerParams(vmem_limit_bytes=16 * MIB),
        cost_estimate=pl.CostEstimate(flops=0, bytes_accessed=13 * MIB, transcendentals=0),
        name="unpack",
    )(packed)


def lay_out_kernel(parts, blocks, per, numbers_ref, *refs):
    count = len(refs) - 3
    joint_ref, dense_ref, vectors_ref = refs[count:]
    lanes = vectors_ref.shape[1]
    columns = parts * blocks
    for k in range(count):
        chunk_ref = refs[k]
        rows = pl.ds(pl.multiple_of(numbers_ref[k] * per, per), per)
        for c in range(columns):
            joint_ref[rows, c * lanes : (c + 1) * lanes] = chunk_ref[c * per : (c + 1) * per].astype(F32)
        first = columns * per
        for c in range(dense_ref.shape[1] // lanes):
            start = first + c * per
            dense_ref[rows, c * lanes : (c + 1) * lanes] = chunk_ref[start : start + per].astype(F32)
        first += dense_ref.shape[1] // lanes * per
        rows = pl.ds(pl.multiple_of(numbers_ref[k] * 16, 16), 16)
        vectors_ref[rows, :] = chunk_ref[first : first + 16].astype(F32)


def lay_out(numbers, chunks, parts, blocks, per, joint_shape, dense_shape):
    lanes = chunks[0].shape[1]
    whole = pl.BlockSpec(memory_space=pltpu.VMEM)
    return pl.pallas_call(
        functools.partial(lay_out_kernel, parts, blocks, per),
        in_specs=[pl.BlockSpec(memory_space=pltpu.SMEM)] + [whole] * len(chunks),
        out_specs=[whole] * 3,
        out_shape=[
            jax.ShapeDtypeStruct(joint_shape, F32),
            jax.ShapeDtypeStruct(dense_shape, F32),
            jax.ShapeDtypeStruct((16 * len(chunks), lanes), F32),
        ],
        compiler_params=pltpu.CompilerParams(vmem_limit_bytes=24 * MIB),
        cost_estimate=pl.CostEstimate(flops=0, bytes_accessed=6 * MIB, transcendentals=0),
        name="lay_out",
    )(numbers, *chunks)


def lay_out_wide_kernel(outer_rows, parts, numbers_ref, *refs):
    count = len(refs) - 2
    outer_ref, inner_ref = refs[count:]
    width = outer_ref.shape[1]
    per = inner_ref.shape[0] // count
    for k in range(count):
        start = pl.multiple_of(numbers_ref[k] * outer_rows, outer_rows)
        outer_ref[pl.ds(start, outer_rows), :] = refs[k][:outer_rows].astype(F32)
        rows = pl.ds(pl.multiple_of(numbers_ref[k] * per, per), per)
        for part in range(parts):
            first = outer_rows + part * per
            inner_ref[rows, part * width : (part + 1) * width] = refs[k][first : first + per].astype(F32)


def lay_out_wide(numbers, chunks, outer_rows, parts):
    rows, width = chunks[0].shape
    count = len(chunks)
    per = (rows - outer_rows) // parts
    whole = pl.BlockSpec(memory_space=pltpu.VMEM)
    return pl.pallas_call(
        functools.partial(lay_out_wide_kernel, outer_rows, parts),
        in_specs=[pl.BlockSpec(memory_space=pltpu.SMEM)] + [whole] * count,
        out_specs=[whole] * 2,
        out_shape=[
            jax.ShapeDtypeStruct((count * outer_rows, width), F32),
            jax.ShapeDtypeStruct((count * per, parts * width), F32),
        ],
        compiler_params=pltpu.CompilerParams(vmem_limit_bytes=24 * MIB),
        cost_estimate=pl.CostEstimate(flops=0, bytes_accessed=12 * MIB, transcendentals=0),
        name="lay_out_wide",
    )(numbers, *chunks)


def spread_out(part, ctx, each):
    if ctx > part.shape[0]:
        part = jnp.concatenate([part] * (ctx // part.shape[0]), axis=0)
    return lax.all_to_all(part.reshape((ctx, each) + part.shape[1:]), "ctx", 0, 0)


def rotary_tables(token_pos):
    lane = jnp.arange(PAIR, dtype=jnp.int32) % DH
    exponent = (2 * (lane % (ROT // 2))).astype(F32) / ROT
    inverse = 10000.0 ** (-exponent)
    phases = token_pos[:, None] * inverse[None, :]
    turned = (lane < ROT)[None, :]
    sign = jnp.where(lane < ROT // 2, -1.0, 1.0)[None, :]
    return jnp.where(turned, jnp.cos(phases), 1.0), jnp.where(turned, jnp.sin(phases) * sign, 0.0)


def per_device(ctx, fsdp, tokens, cotangent, positions, block_order, joint_weight, joint_bias,
               dense_weight, dense_bias, inner_weight, inner_bias, outer_weight, outer_bias,
               attention_gain, attention_shift, feedforward_gain, feedforward_shift):
    seqs = fsdp
    count = tokens.shape[1]
    block = count // 2
    rows = joint_weight.shape[0]
    heads = H // fsdp
    pairs = heads // 2
    joint_cols = heads * 3 * DH
    inner_cols = inner_weight.shape[1] // fsdp
    all_tokens = seqs * count
    me = lax.axis_index("ctx")

    pos = positions[0]
    table = block_order[0].astype(BF16)
    extra = jnp.stack(
        [
            attention_gain, attention_shift, feedforward_gain, feedforward_shift,
            dense_bias, outer_bias, (pos // 128).astype(BF16), (pos % 128).astype(BF16),
            jnp.pad(table, (0, rows - table.shape[0])),
        ]
    )
    extra = gather_pairs(jnp.pad(extra, ((0, 7), (0, 0))), fsdp).astype(F32)
    both = gather_pairs(jnp.concatenate([tokens, cotangent], axis=0), fsdp)
    joint_local = lax.all_to_all(
        joint_weight.reshape(rows, fsdp, joint_cols).transpose(1, 0, 2), "fsdp", 0, 0
    ).reshape(D, joint_cols)
    upstream = both[:, 1].reshape(all_tokens, D)

    params = extra[:, :4].transpose(1, 0, 2).reshape(4, D)
    bias_sum = (extra[:, 4] + extra[:, 5]).reshape(D)
    token_pos = (extra[:, 6] * 128.0 + extra[:, 7]).reshape(all_tokens)
    tables = extra[:, 8, : table.shape[0]].astype(jnp.int32)

    cosine, sine = rotary_tables(token_pos)

    sent, hidden_attn, hidden_ff, normed = project(
        both, params, joint_local, joint_bias[None], dense_weight, cosine, sine, seqs, count, pairs
    )
    jobs = seqs * pairs
    each = max(1, jobs // ctx)
    got = spread_out(sent, ctx, each)
    backs = []
    for k in range(each):
        sequence = (lax.rem(me, jobs) * each + k) // pairs
        order = lax.dynamic_index_in_dim(tables, sequence, 0, keepdims=False)
        out = attend(order, got[:, k].reshape(ctx * count, 4 * PAIR), block, sent)
        backs.append(out.reshape(ctx, count, 4 * PAIR))
    back = backs[0][:, None] if each == 1 else jnp.stack(backs, axis=1)
    inner_local = columns_for_rows(inner_weight, fsdp, nothing(got), nothing(back))

    outer_weight_grad, inner_weight_grad, inner_bias_grad, ff_out, hidden_ff_grad = feed(
        hidden_ff, inner_local, inner_bias[None], outer_weight, upstream
    )
    inner_bias_grad = inner_bias_grad[0]

    per = rows // ctx
    outer_rows = outer_weight.shape[0] // ctx
    inner_terms = inner_weight_grad.reshape(fsdp, ctx, per, inner_cols).transpose(1, 0, 2, 3)
    ff_terms = jnp.concatenate(
        [
            outer_weight_grad.reshape(ctx, outer_rows, D),
            inner_terms.reshape(ctx, fsdp * per, inner_cols),
        ],
        axis=1,
    )
    ff_own = ring_reduce(
        lambda k: lax.dynamic_index_in_dim(ff_terms, k, 0, keepdims=False), "ctx", ctx
    )
    back = lax.all_to_all(back, "ctx", 0, 0)[: jobs // each].reshape(jobs, count, 4 * PAIR)
    joint_grad, mixed = unturn(back, cosine, sine, ff_terms, seqs, count, pairs)

    out_part = (ff_out + dot(mixed, dense_weight)).astype(BF16)
    hidden_attn_grad = dot(joint_grad, joint_local, 1, 1)
    e_part = (params[0] * hidden_attn_grad + params[2] * hidden_ff_grad).astype(BF16)
    parts = lax.all_to_all(
        jnp.concatenate([out_part.reshape(seqs, count, D), e_part.reshape(seqs, count, D)], axis=1),
        "fsdp", 0, 0,
    )

    dense_weight_grad = dot(mixed, upstream, 0, 0).astype(BF16)
    joint_weight_grad = dot(hidden_attn, joint_grad, 0, 0).astype(BF16)
    joint_bias_grad = jnp.sum(joint_grad.astype(F32), axis=0)
    upstream_grad = jnp.sum(upstream.astype(F32), axis=0)

    gains = jnp.stack(
        [
            jnp.sum(hidden_attn_grad * normed.astype(F32), axis=0),
            jnp.sum(hidden_attn_grad, axis=0),
            jnp.sum(hidden_ff_grad * normed.astype(F32), axis=0),
            jnp.sum(hidden_ff_grad, axis=0),
        ]
    ).astype(BF16)
    lanes = 2 * PAIR
    gains = gains.reshape(4, fsdp, ctx, per).transpose(2, 1, 0, 3).reshape(ctx, fsdp, 4 * per)
    gains = jnp.pad(gains, ((0, 0), (0, 0), (0, lanes - 4 * per)))
    my_rows = lax.dynamic_slice_in_dim(
        upstream_grad, lax.axis_index("fsdp") * rows, rows, 0
    )
    small = jnp.concatenate(
        [joint_bias_grad.reshape(ctx, -1), inner_bias_grad.reshape(ctx, -1), my_rows.reshape(ctx, -1)],
        axis=1,
    ).astype(BF16)
    small = jnp.pad(small[:, None], ((0, 0), (0, 31 - fsdp), (0, lanes - small.shape[1])))
    joint_blocks, dense_blocks = joint_cols // lanes, D // lanes
    terms = jnp.concatenate(
        [
            joint_weight_grad.reshape(fsdp, ctx, per, joint_blocks, lanes)
            .transpose(1, 0, 3, 2, 4).reshape(ctx, -1, lanes),
            dense_weight_grad.reshape(ctx, per, dense_blocks, lanes)
            .transpose(0, 2, 1, 3).reshape(ctx, -1, lanes),
            gains,
            small,
        ],
        axis=1,
    )
    own = ring_reduce(lambda k: lax.dynamic_index_in_dim(terms, k, 0, keepdims=False), "ctx", ctx)
    joint_rows = fsdp * joint_blocks * per
    dense_rows = dense_blocks * per
    ahead = joint_rows + dense_rows
    gain_rows = jnp.pad(own[ahead : ahead + fsdp][:, None], ((0, 0), (0, 15), (0, 0)))
    joint_part = lax.dynamic_slice_in_dim(own, nothing(parts), joint_rows, 0)
    late_rows = joint_blocks * per + 16
    exchanged = jnp.concatenate(
        [
            joint_part.reshape(fsdp, joint_blocks * per, lanes),
            gain_rows,
            ff_own[outer_rows:].reshape(fsdp, per, -1, lanes).transpose(0, 2, 1, 3).reshape(
                fsdp, -1, lanes
            ),
        ],
        axis=1,
    )
    exchanged = lax.all_to_all(exchanged, "fsdp", 0, 0)
    inner_own = exchanged[:, late_rows:].reshape(fsdp, -1, per, lanes).transpose(0, 2, 1, 3)
    ff_own = jnp.concatenate(
        [ff_own[:outer_rows], inner_own.reshape(fsdp * per, inner_cols)], axis=0
    )
    if per % 16:
        ff_all = lax.all_gather(ff_own, "ctx", axis=0)
        outer_total, inner_total = unpack(ff_all, outer_rows, fsdp)
    else:
        ff_chunks, ff_numbers = ring_gather(
            ff_own, "ctx", ctx,
            lambda state, chunk, number, part: (state[0] + [chunk], state[1] + [number]),
            ([], []),
        )
        outer_total, inner_total = lay_out_wide(
            jnp.stack(ff_numbers).astype(jnp.int32), ff_chunks, outer_rows, fsdp
        )
    gain_own = jnp.sum(exchanged[:, joint_blocks * per].astype(F32), axis=0).astype(BF16)
    own = jnp.concatenate(
        [
            exchanged[:, : joint_blocks * per].reshape(joint_rows, lanes),
            own[joint_rows:ahead],
            jnp.pad(gain_own[None], ((0, fsdp - 1), (0, 0))),
            own[ahead + fsdp :],
        ],
        axis=0,
    )

    def place_late(state, chunk, number, part):
        joint_state, dense_state, vectors = state
        wide = chunk[:joint_rows].reshape(fsdp, joint_blocks, per, lanes).transpose(2, 0, 1, 3)
        joint_state = lax.dynamic_update_slice_in_dim(
            joint_state, wide.reshape(per, -1).astype(F32), number * per, 0
        )
        wide = chunk[joint_rows:ahead].reshape(dense_blocks, per, lanes).transpose(1, 0, 2)
        dense_state = lax.dynamic_update_slice_in_dim(
            dense_state, wide.reshape(per, -1).astype(F32), number * per, 0
        )
        pieces = jnp.stack([chunk[ahead + fsdp], chunk[ahead]])[None]
        vectors = lax.dynamic_update_slice_in_dim(vectors, pieces.astype(F32), number, 0)
        return joint_state, dense_state, vectors

    if per % 16:
        joint_total, dense_total, vectors = ring_gather(
            own, "ctx", ctx, place_late,
            (jnp.zeros(joint_weight.shape, F32), jnp.zeros(dense_weight.shape, F32),
             jnp.zeros((ctx, 2, lanes), F32)),
        )
    else:
        chunks, numbers = ring_gather(
            own, "ctx", ctx,
            lambda state, chunk, number, part: (state[0] + [chunk], state[1] + [number]),
            ([], []),
        )
        joint_total, dense_total, vectors = lay_out(
            jnp.stack(numbers).astype(jnp.int32), chunks, fsdp, joint_blocks, per,
            joint_weight.shape, dense_weight.shape,
        )
        vectors = vectors.reshape(ctx, 16, lanes)
        vectors = jnp.stack([vectors[:, fsdp], vectors[:, 0]], axis=1)
    a, b = joint_cols // ctx, inner_cols // ctx
    joint_bias_total = vectors[:, 0, :a].reshape(-1)
    inner_bias_total = vectors[:, 0, a : a + b].reshape(-1)
    upstream_total = vectors[:, 0, a + b : a + b + per].reshape(-1)
    gain_totals = [vectors[:, 1, k * per : (k + 1) * per].reshape(-1) for k in range(4)]

    layer_output = (tokens[0].astype(F32) + bias_sum
                    + jnp.sum(parts[:, :count].astype(F32), axis=0)).astype(BF16)
    e = jnp.sum(parts[:, count:].astype(F32), axis=0)
    mine = tokens[0].astype(F32)
    mine_centered = mine - jnp.mean(mine, axis=-1, keepdims=True)
    mine_spread = lax.rsqrt(jnp.mean(mine_centered * mine_centered, axis=-1, keepdims=True) + EPSILON)
    mine_normed = mine_centered * mine_spread
    tokens_grad = (
        cotangent[0].astype(F32)
        + (e - jnp.mean(e, axis=-1, keepdims=True)
           - mine_normed * jnp.mean(e * mine_normed, axis=-1, keepdims=True)) * mine_spread
    ).astype(BF16)

    return (
        layer_output[None], tokens_grad[None],
        joint_total, joint_bias_total, dense_total, upstream_total,
        inner_total, inner_bias_total, outer_total, upstream_total,
        gain_totals[0], gain_totals[1], gain_totals[2], gain_totals[3],
    )


def solution(mesh):
    tokens = P("fsdp", "ctx", None)
    weight = P("fsdp", None)
    vector = P("fsdp")
    return jax.shard_map(
        functools.partial(per_device, mesh.shape["ctx"], mesh.shape["fsdp"]),
        mesh=mesh,
        in_specs=(tokens, tokens, P("fsdp", "ctx"), weight) + (weight, vector) * 4 + (vector,) * 4,
        out_specs=(tokens, tokens) + (weight, vector) * 4 + (vector,) * 4,
        check_vma=False,
    )
```

```python
import functools
import math

import jax
import jax.numpy as jnp
from jax import lax
from jax.experimental import pallas as pl
from jax.experimental.pallas import tpu as pltpu
from jax.sharding import PartitionSpec as P

D = 1024
H = 16
DH = 64
ROT = 16
PAIR = 2 * DH
EPSILON = 1e-05
MASKED = -1e30
SCALE = DH ** (-0.5)
LOG2E = math.log2(math.e)
BF16 = jnp.bfloat16
F32 = jnp.float32
MIB = 1024 * 1024


def dot(left, right, left_dim=1, right_dim=0):
    return lax.dot_general(
        left, right, (((left_dim,), (right_dim,)), ((), ())), preferred_element_type=F32
    )


def ring_order(count):
    return list(range(0, count, 2)) + list(range(1, count, 2))[::-1]


def ring_steps(axis, count):
    order = ring_order(count)
    onward = [(order[k], order[(k + 1) % count]) for k in range(count)]
    back = [(b, a) for a, b in onward]
    places = [0] * count
    for place, index in enumerate(order):
        places[index] = place
    place = jnp.array(places, jnp.int32)[lax.axis_index(axis)]
    return onward, back, place


def ring_reduce(pick, axis, count):
    onward, back, place = ring_steps(axis, count)
    half = count // 2
    far = pick((place + half) % count)
    rows = far.shape[0] // 2
    up = lax.ppermute(far[:rows], axis, onward)
    down = lax.ppermute(far[rows:], axis, back)
    for step in range(2, half + 1):
        mine_up = pick((place + half - step + 1) % count)
        mine_down = pick((place + count - half + step - 1) % count)
        if step == 2:
            mine_up = jnp.concatenate([mine_up[:rows] + up, mine_up[rows:]], axis=0)
            mine_down = jnp.concatenate([mine_down[:rows], mine_down[rows:] + down], axis=0)
        else:
            mine_up = mine_up + up
            mine_down = mine_down + down
        up = lax.ppermute(mine_up, axis, onward)
        down = lax.ppermute(mine_down, axis, back)
    own = pick(place).astype(F32)
    return (own + up.astype(F32) + down.astype(F32)).astype(BF16)


def ring_gather(own, axis, count, place_chunk, state, zero=0):
    onward, back, place = ring_steps(axis, count)
    half = count // 2
    rows = own.shape[0] // 2
    state = place_chunk(state, own, place, 0)
    up = down = own
    for step in range(1, half):
        up = lax.ppermute(up, axis, onward)
        down = lax.ppermute(down, axis, back)
        state = place_chunk(state, up, (place + count - step) % count, 0)
        state = place_chunk(state, down, (place + step) % count, 0)
    up = lax.ppermute(lax.dynamic_slice_in_dim(up, zero, rows, 0), axis, onward)
    down = lax.ppermute(lax.dynamic_slice_in_dim(down, zero + rows, rows, 0), axis, back)
    return place_chunk(state, jnp.concatenate([up, down], axis=0), (place + half) % count, 0)


def nothing(array):
    value = array.reshape(-1)[0].astype(jnp.int32)
    return jnp.minimum(jnp.abs(value), 0)


def gather_pairs(own, count):
    if count != 4:
        return lax.all_gather(own, "fsdp", axis=0)
    index = lax.axis_index("fsdp")
    across = lax.ppermute(own, "fsdp", [(k, k ^ 2) for k in range(4)])
    first = index < 2
    pair = jnp.stack([jnp.where(first, own, across), jnp.where(first, across, own)])
    other = lax.ppermute(pair, "fsdp", [(k, k ^ 1) for k in range(4)])
    even = index % 2 == 0
    return jnp.stack([jnp.where(even, pair, other), jnp.where(even, other, pair)], axis=1).reshape(
        (4,) + own.shape
    )


def columns_for_rows(weight, count, zero, later):
    rows, columns = weight.shape
    part = columns // count
    if count != 4:
        parts = weight.reshape(rows, count, part).transpose(1, 0, 2)
        return lax.all_to_all(parts, "fsdp", 0, 0).reshape(count * rows, part)
    index = lax.axis_index("fsdp")
    chip, core = index // 2, index % 2
    mine = lax.dynamic_slice_in_dim(weight, chip * 2 * part, 2 * part, 1)
    theirs = lax.dynamic_slice_in_dim(weight, (1 - chip) * 2 * part + zero, 2 * part, 1)
    across = lax.ppermute(theirs, "fsdp", [(k, k ^ 2) for k in range(4)])
    low = chip == 0
    pair = jnp.stack([jnp.where(low, mine, across), jnp.where(low, across, mine)])
    even = core == 0
    other = lax.ppermute(
        lax.dynamic_slice_in_dim(pair, (1 - core) * part + later, part, 2),
        "fsdp",
        [(k, k ^ 1) for k in range(4)],
    )
    kept = lax.dynamic_slice_in_dim(pair, core * part, part, 2)
    return jnp.stack(
        [jnp.where(even, kept, other), jnp.where(even, other, kept)], axis=1
    ).reshape(count * rows, part)


def turn(heads, cosine, sine):
    lane = lax.broadcasted_iota(jnp.int32, heads.shape, 1) % DH
    partner = jnp.where(
        lane < ROT // 2,
        pltpu.roll(heads, PAIR - ROT // 2, 1),
        pltpu.roll(heads, ROT // 2, 1),
    )
    return heads * cosine + partner * sine


def project_kernel(tokens_ref, upstream_ref, params_ref, weight_ref, bias_ref, dense_ref, cos_ref,
                   sin_ref, out_ref, attn_ref, ff_ref, normed_ref):
    @pl.when(pl.program_id(1) == 0)
    def norm():
        inputs = tokens_ref[0, 0].astype(F32)
        centered = inputs - jnp.mean(inputs, axis=-1, keepdims=True)
        variance = jnp.mean(centered * centered, axis=-1, keepdims=True)
        normed = centered * lax.rsqrt(variance + EPSILON)
        normed_ref[...] = normed.astype(BF16)
        attn_ref[...] = (normed * params_ref[0:1] + params_ref[1:2]).astype(BF16)
        ff_ref[...] = (normed * params_ref[2:3] + params_ref[3:4]).astype(BF16)

    joint = dot(attn_ref[...], weight_ref[...]) + bias_ref[...].astype(F32)
    low = lax.broadcasted_iota(jnp.int32, (joint.shape[0], PAIR), 1) < DH
    one, two, three = joint[:, :PAIR], joint[:, PAIR : 2 * PAIR], joint[:, 2 * PAIR :]
    query = jnp.where(low, one, two)
    key = pltpu.roll(jnp.where(low, three, one), DH, 1)
    value = jnp.where(low, two, three)
    cosine, sine = cos_ref[...], sin_ref[...]
    out_ref[0, :, :PAIR] = turn(query, cosine, sine).astype(BF16)
    out_ref[0, :, PAIR : 2 * PAIR] = turn(key, cosine, sine).astype(BF16)
    out_ref[0, :, 2 * PAIR : 3 * PAIR] = value.astype(BF16)
    out_ref[0, :, 3 * PAIR :] = dot(upstream_ref[0, 0], dense_ref[...], 1, 1).astype(BF16)


def project(both, params, weight, bias, dense, cosine, sine, seqs, tokens, pairs):
    wide = jax.ShapeDtypeStruct((seqs * tokens, D), BF16)
    rows = pl.BlockSpec((tokens, D), lambda s, p: (s, 0))
    return pl.pallas_call(
        project_kernel,
        grid=(seqs, pairs),
        in_specs=[
            pl.BlockSpec((1, 1, tokens, D), lambda s, p: (s, 0, 0, 0)),
            pl.BlockSpec((1, 1, tokens, D), lambda s, p: (s, 1, 0, 0)),
            pl.BlockSpec((4, D), lambda s, p: (0, 0)),
            pl.BlockSpec((D, 3 * PAIR), lambda s, p: (0, p)),
            pl.BlockSpec((1, 3 * PAIR), lambda s, p: (0, p)),
            pl.BlockSpec((PAIR, D), lambda s, p: (p, 0)),
            pl.BlockSpec((tokens, PAIR), lambda s, p: (s, 0)),
            pl.BlockSpec((tokens, PAIR), lambda s, p: (s, 0)),
        ],
        out_specs=[
            pl.BlockSpec((1, tokens, 4 * PAIR), lambda s, p: (s * pairs + p, 0, 0)),
            rows,
            rows,
            rows,
        ],
        out_shape=[
            jax.ShapeDtypeStruct((seqs * pairs, tokens, 4 * PAIR), BF16), wide, wide, wide,
        ],
        compiler_params=pltpu.CompilerParams(vmem_limit_bytes=40 * MIB),
        cost_estimate=pl.CostEstimate(
            flops=3 * seqs * pairs * tokens * D * 4 * PAIR,
            bytes_accessed=16 * MIB,
            transcendentals=0,
        ),
        name="project",
    )(both, both, params, weight, bias, dense, cosine, sine)


def unturn_kernel(back_ref, cos_ref, sin_ref, first_ref, grad_ref, mixed_ref):
    cosine, sine = cos_ref[...], sin_ref[...]
    query = turn(back_ref[0, :, PAIR : 2 * PAIR].astype(F32), cosine, -sine)
    key = turn(back_ref[0, :, 2 * PAIR : 3 * PAIR].astype(F32), cosine, -sine)
    value = back_ref[0, :, 3 * PAIR :].astype(F32)
    low = lax.broadcasted_iota(jnp.int32, query.shape, 1) < DH
    key = pltpu.roll(key, DH, 1)
    grad_ref[:, :PAIR] = jnp.where(low, query, key).astype(BF16)
    grad_ref[:, PAIR : 2 * PAIR] = jnp.where(low, value, query).astype(BF16)
    grad_ref[:, 2 * PAIR :] = jnp.where(low, key, value).astype(BF16)
    mixed_ref[...] = back_ref[0, :, :PAIR]


def unturn(back, cosine, sine, first, seqs, tokens, pairs):
    return pl.pallas_call(
        unturn_kernel,
        grid=(seqs, pairs),
        in_specs=[
            pl.BlockSpec((1, tokens, 4 * PAIR), lambda s, p: (s * pairs + p, 0, 0)),
            pl.BlockSpec((tokens, PAIR), lambda s, p: (s, 0)),
            pl.BlockSpec((tokens, PAIR), lambda s, p: (s, 0)),
            pl.BlockSpec(memory_space=pl.ANY),
        ],
        out_specs=[
            pl.BlockSpec((tokens, 3 * PAIR), lambda s, p: (s, p)),
            pl.BlockSpec((tokens, PAIR), lambda s, p: (s, p)),
        ],
        out_shape=[
            jax.ShapeDtypeStruct((seqs * tokens, pairs * 3 * PAIR), BF16),
            jax.ShapeDtypeStruct((seqs * tokens, pairs * PAIR), BF16),
        ],
        compiler_params=pltpu.CompilerParams(vmem_limit_bytes=32 * MIB),
        cost_estimate=pl.CostEstimate(flops=8 * MIB, bytes_accessed=5 * MIB, transcendentals=0),
        name="unturn",
    )(back, cosine, sine, first)


def attend_kernel(tile, block, unrolled, order_ref, in_ref, first_ref, out_ref, sorted_ref, flipped_ref,
                  score_ref, prob_ref, mixed_ref, dq_ref, dk_ref, dv_ref):
    head = pl.program_id(0)
    length = in_ref.shape[0]
    tiles = length // tile
    blocks = length // block

    def loop(count, body, carry):
        if unrolled:
            for index in range(count):
                carry = body(index, carry)
            return carry
        return lax.fori_loop(0, count, body, carry)

    def span(index, size):
        start = index * size
        if not isinstance(start, int):
            start = pl.multiple_of(start, size)
        return pl.ds(start, size)

    @pl.when(head == 0)
    def prepare():
        def one(index, carry):
            sorted_ref[span(order_ref[index], block), :] = in_ref[span(index, block), :]
            return carry

        loop(blocks, one, 0)

        def flip(index, carry):
            flipped_ref[:, span(index, tile)] = sorted_ref[span(index, tile), :].T
            return carry

        loop(tiles, flip, 0)
        dk_ref[...] = jnp.zeros_like(dk_ref)
        dv_ref[...] = jnp.zeros_like(dv_ref)

    first = pl.multiple_of(head * DH, DH)

    def padded(rows):
        rows = rows.astype(F32)
        zero = jnp.zeros_like(rows)
        upper = jnp.where(head == 0, rows, zero)
        lower = jnp.where(head == 0, zero, rows)
        return jnp.concatenate([upper, lower], axis=0).astype(BF16)

    def one_tile(i, carry):
        query = padded(flipped_ref[pl.ds(first, DH), span(i, tile)])

        def score(j, top):
            part = dot(sorted_ref[span(j, tile), PAIR : 2 * PAIR], query)
            if not (unrolled and j < i):
                keys = j * tile + lax.broadcasted_iota(jnp.int32, part.shape, 0)
                queries = i * tile + lax.broadcasted_iota(jnp.int32, part.shape, 1)
                part = jnp.where(keys <= queries, part, MASKED)
            score_ref[span(j, tile), :] = part
            return jnp.maximum(top, jnp.max(part, axis=0, keepdims=True))

        top = loop(i + 1, score, jnp.full((1, tile), -3e38, F32))
        shift = top * (SCALE * LOG2E)

        def mix(j, status):
            total, mixed = status
            prob = jnp.exp2(score_ref[span(j, tile), :] * (SCALE * LOG2E) - shift)
            low = prob.astype(BF16)
            prob_ref[span(j, tile), :] = low
            total = total + jnp.sum(prob, axis=0, keepdims=True)
            values = flipped_ref[pl.ds(2 * PAIR + first, DH), span(j, tile)]
            return total, mixed + dot(values, low)

        total, mixed = loop(
            i + 1, mix, (jnp.zeros((1, tile), F32), jnp.zeros((DH, tile), F32))
        )
        inverse = 1.0 / total
        mixed = mixed * inverse
        mixed_ref[pl.ds(first, DH), span(i, tile)] = mixed
        grad = flipped_ref[pl.ds(3 * PAIR + first, DH), span(i, tile)].astype(F32) * inverse
        grad = grad.astype(BF16)
        delta = jnp.sum(grad.astype(F32) * mixed, axis=0, keepdims=True)
        grad = padded(grad)

        def pull(j, dq):
            low = prob_ref[span(j, tile), :]
            prob_grad = dot(sorted_ref[span(j, tile), 2 * PAIR : 3 * PAIR], grad)
            score_grad = (low.astype(F32) * (prob_grad - delta)).astype(BF16)
            dv_ref[span(j, tile), :] += dot(low, grad, 1, 1)
            dk_ref[span(j, tile), :] += dot(score_grad, query, 1, 1)
            keys = flipped_ref[pl.ds(PAIR + first, DH), span(j, tile)]
            return dq + dot(keys, score_grad)

        dq_ref[pl.ds(first, DH), span(i, tile)] = loop(i + 1, pull, jnp.zeros((DH, tile), F32))
        return carry

    loop(tiles, one_tile, 0)

    @pl.when(head == pl.num_programs(0) - 1)
    def finish():
        def one(index, carry):
            source = span(order_ref[index], block)
            target = span(index, block)
            out_ref[target, :PAIR] = mixed_ref[:, source].T.astype(BF16)
            out_ref[target, PAIR : 2 * PAIR] = (dq_ref[:, source].T * SCALE).astype(BF16)
            out_ref[target, 2 * PAIR : 3 * PAIR] = (dk_ref[source, :] * SCALE).astype(BF16)
            out_ref[target, 3 * PAIR :] = dv_ref[source, :].astype(BF16)
            return carry

        loop(blocks, one, 0)


def attend(order, packed, block, first):
    length = packed.shape[0]
    unrolled = length <= 2048
    tile = 256 if unrolled else 128
    return pl.pallas_call(
        functools.partial(attend_kernel, tile, block, unrolled),
        grid=(2,),
        in_specs=[
            pl.BlockSpec(memory_space=pltpu.SMEM),
            pl.BlockSpec(memory_space=pltpu.VMEM),
            pl.BlockSpec(memory_space=pl.ANY),
        ],
        out_specs=pl.BlockSpec(memory_space=pltpu.VMEM),
        out_shape=jax.ShapeDtypeStruct((length, 4 * PAIR), BF16),
        scratch_shapes=[
            pltpu.VMEM((length, 4 * PAIR), BF16),
            pltpu.VMEM((4 * PAIR, length), BF16),
            pltpu.VMEM((length, tile), F32),
            pltpu.VMEM((length, tile), BF16),
            pltpu.VMEM((PAIR, length), F32),
            pltpu.VMEM((PAIR, length), F32),
            pltpu.VMEM((length, PAIR), F32),
            pltpu.VMEM((length, PAIR), F32),
        ],
        compiler_params=pltpu.CompilerParams(
            vmem_limit_bytes=(40 if unrolled else 60) * MIB,
            dimension_semantics=("arbitrary",),
        ),
        cost_estimate=pl.CostEstimate(
            flops=56 * length * length * PAIR, bytes_accessed=4 * MIB, transcendentals=0
        ),
        name="attend",
    )(order, packed, first)


def feed_kernel(hidden_ref, inner_ref, bias_ref, outer_ref, upstream_ref,
                outer_grad_ref, inner_grad_ref, bias_grad_ref, out_ref, hidden_grad_ref):
    step = pl.program_id(0)
    hidden, upstream = hidden_ref[...], upstream_ref[...]
    inner = dot(hidden, inner_ref[...]) + bias_ref[...].astype(F32)
    share = 0.5 + 0.5 * lax.erf(inner * (0.5 ** 0.5))
    density = jnp.exp(inner * inner * -0.5) * (1.0 / math.sqrt(2.0 * math.pi))
    activated = (inner * share).astype(BF16)
    slope = share + inner * density
    inner_grad = (dot(upstream, outer_ref[...], 1, 1) * slope).astype(BF16)
    outer_grad_ref[...] = dot(activated, upstream, 0, 0).astype(BF16)
    inner_grad_ref[...] = dot(hidden, inner_grad, 0, 0).astype(BF16)
    bias_grad_ref[...] = jnp.sum(inner_grad.astype(F32), axis=0, keepdims=True)
    out = dot(activated, outer_ref[...])
    hidden_grad = dot(inner_grad, inner_ref[...], 1, 1)

    @pl.when(step == 0)
    def begin():
        out_ref[...] = out
        hidden_grad_ref[...] = hidden_grad

    @pl.when(step > 0)
    def add():
        out_ref[...] += out
        hidden_grad_ref[...] += hidden_grad


def feed(hidden, inner, bias, outer, upstream):
    tokens, columns = hidden.shape[0], inner.shape[1]
    tile = 256
    whole = pl.BlockSpec((tokens, D), lambda t: (0, 0))
    return pl.pallas_call(
        feed_kernel,
        grid=(columns // tile,),
        in_specs=[
            whole,
            pl.BlockSpec((D, tile), lambda t: (0, t)),
            pl.BlockSpec((1, tile), lambda t: (0, t)),
            pl.BlockSpec((tile, D), lambda t: (t, 0)),
            whole,
        ],
        out_specs=[
            pl.BlockSpec((tile, D), lambda t: (t, 0)),
            pl.BlockSpec((D, tile), lambda t: (0, t)),
            pl.BlockSpec((1, tile), lambda t: (0, t)),
            whole,
            whole,
        ],
        out_shape=[
            jax.ShapeDtypeStruct((columns, D), BF16),
            jax.ShapeDtypeStruct((D, columns), BF16),
            jax.ShapeDtypeStruct((1, columns), F32),
            jax.ShapeDtypeStruct((tokens, D), F32),
            jax.ShapeDtypeStruct((tokens, D), F32),
        ],
        compiler_params=pltpu.CompilerParams(vmem_limit_bytes=48 * MIB),
        cost_estimate=pl.CostEstimate(
            flops=0, bytes_accessed=0, transcendentals=0
        ),
        name="feed",
    )(hidden, inner, bias, outer, upstream)


def unpack_kernel(outer_rows, parts, in_ref, outer_ref, inner_ref):
    per = inner_ref.shape[0]
    width = in_ref.shape[2]
    outer_ref[...] = in_ref[0, :outer_rows].astype(F32)
    for part in range(parts):
        start = outer_rows + part * per
        inner_ref[:, part * width : (part + 1) * width] = in_ref[0, start : start + per].astype(F32)


def unpack(packed, outer_rows, parts):
    count, rows, width = packed.shape
    per = (rows - outer_rows) // parts
    if per % 16:
        outer = packed[:, :outer_rows].reshape(-1, width).astype(F32)
        inner = packed[:, outer_rows:].reshape(count, parts, per, width).transpose(0, 2, 1, 3)
        return outer, inner.reshape(count * per, -1).astype(F32)
    return pl.pallas_call(
        functools.partial(unpack_kernel, outer_rows, parts),
        grid=(count,),
        in_specs=[pl.BlockSpec((1, rows, width), lambda c: (c, 0, 0))],
        out_specs=[
            pl.BlockSpec((outer_rows, width), lambda c: (c, 0)),
            pl.BlockSpec((per, parts * width), lambda c: (c, 0)),
        ],
        out_shape=[
            jax.ShapeDtypeStruct((count * outer_rows, width), F32),
            jax.ShapeDtypeStruct((count * per, parts * width), F32),
        ],
        compiler_params=pltpu.CompilerParams(vmem_limit_bytes=16 * MIB),
        cost_estimate=pl.CostEstimate(flops=0, bytes_accessed=13 * MIB, transcendentals=0),
        name="unpack",
    )(packed)


def lay_out_kernel(parts, blocks, per, numbers_ref, *refs):
    count = len(refs) - 3
    joint_ref, dense_ref, vectors_ref = refs[count:]
    lanes = vectors_ref.shape[1]
    columns = parts * blocks
    for k in range(count):
        chunk_ref = refs[k]
        rows = pl.ds(pl.multiple_of(numbers_ref[k] * per, per), per)
        for c in range(columns):
            joint_ref[rows, c * lanes : (c + 1) * lanes] = chunk_ref[c * per : (c + 1) * per].astype(F32)
        first = columns * per
        for c in range(dense_ref.shape[1] // lanes):
            start = first + c * per
            dense_ref[rows, c * lanes : (c + 1) * lanes] = chunk_ref[start : start + per].astype(F32)
        first += dense_ref.shape[1] // lanes * per
        rows = pl.ds(pl.multiple_of(numbers_ref[k] * 16, 16), 16)
        vectors_ref[rows, :] = chunk_ref[first : first + 16].astype(F32)


def lay_out(numbers, chunks, parts, blocks, per, joint_shape, dense_shape):
    lanes = chunks[0].shape[1]
    whole = pl.BlockSpec(memory_space=pltpu.VMEM)
    return pl.pallas_call(
        functools.partial(lay_out_kernel, parts, blocks, per),
        in_specs=[pl.BlockSpec(memory_space=pltpu.SMEM)] + [whole] * len(chunks),
        out_specs=[whole] * 3,
        out_shape=[
            jax.ShapeDtypeStruct(joint_shape, F32),
            jax.ShapeDtypeStruct(dense_shape, F32),
            jax.ShapeDtypeStruct((16 * len(chunks), lanes), F32),
        ],
        compiler_params=pltpu.CompilerParams(vmem_limit_bytes=24 * MIB),
        cost_estimate=pl.CostEstimate(flops=0, bytes_accessed=6 * MIB, transcendentals=0),
        name="lay_out",
    )(numbers, *chunks)


def lay_out_wide_kernel(outer_rows, parts, numbers_ref, *refs):
    count = len(refs) - 2
    outer_ref, inner_ref = refs[count:]
    width = outer_ref.shape[1]
    per = inner_ref.shape[0] // count
    for k in range(count):
        start = pl.multiple_of(numbers_ref[k] * outer_rows, outer_rows)
        outer_ref[pl.ds(start, outer_rows), :] = refs[k][:outer_rows].astype(F32)
        rows = pl.ds(pl.multiple_of(numbers_ref[k] * per, per), per)
        for part in range(parts):
            first = outer_rows + part * per
            inner_ref[rows, part * width : (part + 1) * width] = refs[k][first : first + per].astype(F32)


def lay_out_wide(numbers, chunks, outer_rows, parts):
    rows, width = chunks[0].shape
    count = len(chunks)
    per = (rows - outer_rows) // parts
    whole = pl.BlockSpec(memory_space=pltpu.VMEM)
    return pl.pallas_call(
        functools.partial(lay_out_wide_kernel, outer_rows, parts),
        in_specs=[pl.BlockSpec(memory_space=pltpu.SMEM)] + [whole] * count,
        out_specs=[whole] * 2,
        out_shape=[
            jax.ShapeDtypeStruct((count * outer_rows, width), F32),
            jax.ShapeDtypeStruct((count * per, parts * width), F32),
        ],
        compiler_params=pltpu.CompilerParams(vmem_limit_bytes=24 * MIB),
        cost_estimate=pl.CostEstimate(flops=0, bytes_accessed=12 * MIB, transcendentals=0),
        name="lay_out_wide",
    )(numbers, *chunks)


def spread_out(part, ctx, each):
    if ctx > part.shape[0]:
        part = jnp.concatenate([part] * (ctx // part.shape[0]), axis=0)
    return lax.all_to_all(part.reshape((ctx, each) + part.shape[1:]), "ctx", 0, 0)


def rotary_tables(token_pos):
    lane = jnp.arange(PAIR, dtype=jnp.int32) % DH
    exponent = (2 * (lane % (ROT // 2))).astype(F32) / ROT
    inverse = 10000.0 ** (-exponent)
    phases = token_pos[:, None] * inverse[None, :]
    turned = (lane < ROT)[None, :]
    sign = jnp.where(lane < ROT // 2, -1.0, 1.0)[None, :]
    return jnp.where(turned, jnp.cos(phases), 1.0), jnp.where(turned, jnp.sin(phases) * sign, 0.0)


def per_device(ctx, fsdp, tokens, cotangent, positions, block_order, joint_weight, joint_bias,
               dense_weight, dense_bias, inner_weight, inner_bias, outer_weight, outer_bias,
               attention_gain, attention_shift, feedforward_gain, feedforward_shift):
    seqs = fsdp
    count = tokens.shape[1]
    block = count // 2
    rows = joint_weight.shape[0]
    heads = H // fsdp
    pairs = heads // 2
    joint_cols = heads * 3 * DH
    inner_cols = inner_weight.shape[1] // fsdp
    all_tokens = seqs * count
    me = lax.axis_index("ctx")

    pos = positions[0]
    table = block_order[0].astype(BF16)
    extra = jnp.stack(
        [
            attention_gain, attention_shift, feedforward_gain, feedforward_shift,
            dense_bias, outer_bias, (pos // 128).astype(BF16), (pos % 128).astype(BF16),
            jnp.pad(table, (0, rows - table.shape[0])),
        ]
    )
    extra = gather_pairs(jnp.pad(extra, ((0, 7), (0, 0))), fsdp).astype(F32)
    both = gather_pairs(jnp.concatenate([tokens, cotangent], axis=0), fsdp)
    joint_local = lax.all_to_all(
        joint_weight.reshape(rows, fsdp, joint_cols).transpose(1, 0, 2), "fsdp", 0, 0
    ).reshape(D, joint_cols)
    upstream = both[:, 1].reshape(all_tokens, D)

    params = extra[:, :4].transpose(1, 0, 2).reshape(4, D)
    bias_sum = (extra[:, 4] + extra[:, 5]).reshape(D)
    token_pos = (extra[:, 6] * 128.0 + extra[:, 7]).reshape(all_tokens)
    tables = extra[:, 8, : table.shape[0]].astype(jnp.int32)

    cosine, sine = rotary_tables(token_pos)

    sent, hidden_attn, hidden_ff, normed = project(
        both, params, joint_local, joint_bias[None], dense_weight, cosine, sine, seqs, count, pairs
    )
    jobs = seqs * pairs
    each = max(1, jobs // ctx)
    got = spread_out(sent, ctx, each)
    backs = []
    for k in range(each):
        sequence = (lax.rem(me, jobs) * each + k) // pairs
        order = lax.dynamic_index_in_dim(tables, sequence, 0, keepdims=False)
        out = attend(order, got[:, k].reshape(ctx * count, 4 * PAIR), block, sent)
        backs.append(out.reshape(ctx, count, 4 * PAIR))
    back = backs[0][:, None] if each == 1 else jnp.stack(backs, axis=1)
    inner_local = columns_for_rows(inner_weight, fsdp, nothing(got), nothing(back))

    outer_weight_grad, inner_weight_grad, inner_bias_grad, ff_out, hidden_ff_grad = feed(
        hidden_ff, inner_local, inner_bias[None], outer_weight, upstream
    )
    inner_bias_grad = inner_bias_grad[0]

    per = rows // ctx
    outer_rows = outer_weight.shape[0] // ctx
    inner_terms = inner_weight_grad.reshape(fsdp, ctx, per, inner_cols).transpose(1, 0, 2, 3)
    ff_terms = jnp.concatenate(
        [
            outer_weight_grad.reshape(ctx, outer_rows, D),
            inner_terms.reshape(ctx, fsdp * per, inner_cols),
        ],
        axis=1,
    )
    ff_own = ring_reduce(
        lambda k: lax.dynamic_index_in_dim(ff_terms, k, 0, keepdims=False), "ctx", ctx
    )
    back = lax.all_to_all(back, "ctx", 0, 0)[: jobs // each].reshape(jobs, count, 4 * PAIR)
    joint_grad, mixed = unturn(back, cosine, sine, ff_terms, seqs, count, pairs)

    out_part = (ff_out + dot(mixed, dense_weight)).astype(BF16)
    hidden_attn_grad = dot(joint_grad, joint_local, 1, 1)
    e_part = (params[0] * hidden_attn_grad + params[2] * hidden_ff_grad).astype(BF16)
    parts = lax.all_to_all(
        jnp.concatenate([out_part.reshape(seqs, count, D), e_part.reshape(seqs, count, D)], axis=1),
        "fsdp", 0, 0,
    )

    dense_weight_grad = dot(mixed, upstream, 0, 0).astype(BF16)
    joint_weight_grad = dot(hidden_attn, joint_grad, 0, 0).astype(BF16)
    joint_bias_grad = jnp.sum(joint_grad.astype(F32), axis=0)
    upstream_grad = jnp.sum(upstream.astype(F32), axis=0)

    gains = jnp.stack(
        [
            jnp.sum(hidden_attn_grad * normed.astype(F32), axis=0),
            jnp.sum(hidden_attn_grad, axis=0),
            jnp.sum(hidden_ff_grad * normed.astype(F32), axis=0),
            jnp.sum(hidden_ff_grad, axis=0),
        ]
    ).astype(BF16)
    lanes = 2 * PAIR
    gains = gains.reshape(4, fsdp, ctx, per).transpose(2, 1, 0, 3).reshape(ctx, fsdp, 4 * per)
    gains = jnp.pad(gains, ((0, 0), (0, 0), (0, lanes - 4 * per)))
    my_rows = lax.dynamic_slice_in_dim(
        upstream_grad, lax.axis_index("fsdp") * rows, rows, 0
    )
    small = jnp.concatenate(
        [joint_bias_grad.reshape(ctx, -1), inner_bias_grad.reshape(ctx, -1), my_rows.reshape(ctx, -1)],
        axis=1,
    ).astype(BF16)
    small = jnp.pad(small[:, None], ((0, 0), (0, 31 - fsdp), (0, lanes - small.shape[1])))
    joint_blocks, dense_blocks = joint_cols // lanes, D // lanes
    terms = jnp.concatenate(
        [
            joint_weight_grad.reshape(fsdp, ctx, per, joint_blocks, lanes)
            .transpose(1, 0, 3, 2, 4).reshape(ctx, -1, lanes),
            dense_weight_grad.reshape(ctx, per, dense_blocks, lanes)
            .transpose(0, 2, 1, 3).reshape(ctx, -1, lanes),
            gains,
            small,
        ],
        axis=1,
    )
    own = ring_reduce(lambda k: lax.dynamic_index_in_dim(terms, k, 0, keepdims=False), "ctx", ctx)
    joint_rows = fsdp * joint_blocks * per
    dense_rows = dense_blocks * per
    ahead = joint_rows + dense_rows
    gain_rows = jnp.pad(own[ahead : ahead + fsdp][:, None], ((0, 0), (0, 15), (0, 0)))
    joint_part = own[:joint_rows]
    late_rows = joint_blocks * per + 16
    exchanged = jnp.concatenate(
        [
            joint_part.reshape(fsdp, joint_blocks * per, lanes),
            gain_rows,
            ff_own[outer_rows:].reshape(fsdp, per, -1, lanes).transpose(0, 2, 1, 3).reshape(
                fsdp, -1, lanes
            ),
        ],
        axis=1,
    )
    exchanged = lax.all_to_all(exchanged, "fsdp", 0, 0)
    inner_own = exchanged[:, late_rows:].reshape(fsdp, -1, per, lanes).transpose(0, 2, 1, 3)
    ff_own = jnp.concatenate(
        [ff_own[:outer_rows], inner_own.reshape(fsdp * per, inner_cols)], axis=0
    )
    if per % 16:
        ff_all = lax.all_gather(ff_own, "ctx", axis=0)
        outer_total, inner_total = unpack(ff_all, outer_rows, fsdp)
    else:
        ff_chunks, ff_numbers = ring_gather(
            ff_own, "ctx", ctx,
            lambda state, chunk, number, part: (state[0] + [chunk], state[1] + [number]),
            ([], []),
        )
        outer_total, inner_total = lay_out_wide(
            jnp.stack(ff_numbers).astype(jnp.int32), ff_chunks, outer_rows, fsdp
        )
    gain_own = jnp.sum(exchanged[:, joint_blocks * per].astype(F32), axis=0).astype(BF16)
    own = jnp.concatenate(
        [
            exchanged[:, : joint_blocks * per].reshape(joint_rows, lanes),
            own[joint_rows:ahead],
            jnp.pad(gain_own[None], ((0, fsdp - 1), (0, 0))),
            own[ahead + fsdp :],
        ],
        axis=0,
    )

    def place_late(state, chunk, number, part):
        joint_state, dense_state, vectors = state
        wide = chunk[:joint_rows].reshape(fsdp, joint_blocks, per, lanes).transpose(2, 0, 1, 3)
        joint_state = lax.dynamic_update_slice_in_dim(
            joint_state, wide.reshape(per, -1).astype(F32), number * per, 0
        )
        wide = chunk[joint_rows:ahead].reshape(dense_blocks, per, lanes).transpose(1, 0, 2)
        dense_state = lax.dynamic_update_slice_in_dim(
            dense_state, wide.reshape(per, -1).astype(F32), number * per, 0
        )
        pieces = jnp.stack([chunk[ahead + fsdp], chunk[ahead]])[None]
        vectors = lax.dynamic_update_slice_in_dim(vectors, pieces.astype(F32), number, 0)
        return joint_state, dense_state, vectors

    if per % 16:
        joint_total, dense_total, vectors = ring_gather(
            own, "ctx", ctx, place_late,
            (jnp.zeros(joint_weight.shape, F32), jnp.zeros(dense_weight.shape, F32),
             jnp.zeros((ctx, 2, lanes), F32)),
        )
    else:
        chunks, numbers = ring_gather(
            own, "ctx", ctx,
            lambda state, chunk, number, part: (state[0] + [chunk], state[1] + [number]),
            ([], []),
            nothing(parts),
        )
        joint_total, dense_total, vectors = lay_out(
            jnp.stack(numbers).astype(jnp.int32), chunks, fsdp, joint_blocks, per,
            joint_weight.shape, dense_weight.shape,
        )
        vectors = vectors.reshape(ctx, 16, lanes)
        vectors = jnp.stack([vectors[:, fsdp], vectors[:, 0]], axis=1)
    a, b = joint_cols // ctx, inner_cols // ctx
    joint_bias_total = vectors[:, 0, :a].reshape(-1)
    inner_bias_total = vectors[:, 0, a : a + b].reshape(-1)
    upstream_total = vectors[:, 0, a + b : a + b + per].reshape(-1)
    gain_totals = [vectors[:, 1, k * per : (k + 1) * per].reshape(-1) for k in range(4)]

    layer_output = (tokens[0].astype(F32) + bias_sum
                    + jnp.sum(parts[:, :count].astype(F32), axis=0)).astype(BF16)
    e = jnp.sum(parts[:, count:].astype(F32), axis=0)
    mine = tokens[0].astype(F32)
    mine_centered = mine - jnp.mean(mine, axis=-1, keepdims=True)
    mine_spread = lax.rsqrt(jnp.mean(mine_centered * mine_centered, axis=-1, keepdims=True) + EPSILON)
    mine_normed = mine_centered * mine_spread
    tokens_grad = (
        cotangent[0].astype(F32)
        + (e - jnp.mean(e, axis=-1, keepdims=True)
           - mine_normed * jnp.mean(e * mine_normed, axis=-1, keepdims=True)) * mine_spread
    ).astype(BF16)

    return (
        layer_output[None], tokens_grad[None],
        joint_total, joint_bias_total, dense_total, upstream_total,
        inner_total, inner_bias_total, outer_total, upstream_total,
        gain_totals[0], gain_totals[1], gain_totals[2], gain_totals[3],
    )


def solution(mesh):
    tokens = P("fsdp", "ctx", None)
    weight = P("fsdp", None)
    vector = P("fsdp")
    return jax.shard_map(
        functools.partial(per_device, mesh.shape["ctx"], mesh.shape["fsdp"]),
        mesh=mesh,
        in_specs=(tokens, tokens, P("fsdp", "ctx"), weight) + (weight, vector) * 4 + (vector,) * 4,
        out_specs=(tokens, tokens) + (weight, vector) * 4 + (vector,) * 4,
        check_vma=False,
    )
```
